256 devices in a mesh: ctx: 64 (over z, y, core), head: 4 (over x).
Axes of the slice: x: 4, y: 4, z: 8, core: 2. Of those that a mesh axis runs over, the one named last changes fastest.
Arguments:
- query_rows: bfloat16 [8192, 4096], P('ctx', 'head'), may hold values from -300 to 300
- key_rows: bfloat16 [8192, 4096], P('ctx', 'head'), may hold values from -6 to 6
- value_rows: bfloat16 [8192, 4096], P('ctx', 'head'), may hold values from -6 to 6
- log_decay: float32 [32, 8192], P('head', 'ctx'), may hold values from -1 to 0, as said below
- step_size: float32 [32, 8192], P('head', 'ctx'), may hold values from 0.3 to 6.5
- band_mask: int32 [64, 5], P('ctx'), may hold values from 0 to 1, as said below
- cotangent: bfloat16 [8192, 4096], P('ctx', 'head'), may hold values from -6 to 6
Outputs:
- mixed_out: bfloat16 [8192, 4096], P('ctx', 'head')
- grad_queries: bfloat16 [8192, 4096], P('ctx', 'head')
- grad_keys: bfloat16 [8192, 4096], P('ctx', 'head')
- grad_values: bfloat16 [8192, 4096], P('ctx', 'head')
The draws below stay inside these ranges and needn't reach their ends.
Inputs may be any that keep to these rules, and one draw needn't show every extreme that they name: `log_decay`: strictly negative. band_mask[b, j] = 1 lists the pair of query block b and key block b - j; column 0 is 1 in every row; a listed key block is never negative and is at least b - 4.
All inputs are finite; a program needn't handle non-finite values.
Results may differ from the reference program's by a relative error of at most 0.017.
Values may be sent and summed in bfloat16 or wider, within the bound.
A program may use at most 128 MiB of HBM per device.

```python
import math
import jax
import jax.numpy as jnp
from jax import lax

HEAD_TOTAL = 32
HEAD_DIM = 128
BLK = 128
CYCLE = 4
TOK_DEV = 128
TOKEN_TOTAL = 8192
QBLOCKS = 64
BAND = 5
N_CTX = 64


def query_key_draw(key):
    base_key = jax.random.fold_in(key, 101)
    feat_width = HEAD_TOTAL * HEAD_DIM
    key_draw = jnp.clip(jax.random.normal(jax.random.fold_in(base_key, 1), (TOKEN_TOTAL, feat_width), jnp.float32), -6.0, 6.0)
    query_draw = jnp.clip(jax.random.normal(jax.random.fold_in(base_key, 2), (TOKEN_TOTAL, feat_width), jnp.float32), -6.0, 6.0)
    return (query_draw, key_draw)


def draw_query_rows(key, part):
    return query_key_draw(key)[0].astype(jnp.bfloat16)


def draw_key_rows(key, part):
    return query_key_draw(key)[1].astype(jnp.bfloat16)


def draw_log_decay(key, part):
    head_rank = jax.random.permutation(jax.random.fold_in(key, 1), HEAD_TOTAL)
    fast_share = HEAD_TOTAL // 2
    fast_heads = head_rank < fast_share
    slow_rate = jnp.exp(jax.random.uniform(jax.random.fold_in(key, 2), (HEAD_TOTAL,), jnp.float32, math.log(0.2), math.log(0.8))) / TOKEN_TOTAL
    fast_rate = jnp.exp(jax.random.uniform(jax.random.fold_in(key, 3), (HEAD_TOTAL,), jnp.float32, math.log(1.0 / 50.0), math.log(1.0 / 30.0)))
    head_rate = jnp.where(fast_heads, fast_rate, slow_rate)
    jitter = jnp.exp(jax.random.uniform(jax.random.fold_in(key, 4), (HEAD_TOTAL, TOKEN_TOTAL), jnp.float32, -0.35, 0.35))
    decay_amount = -head_rate[:, None] * jitter
    spike_locations = jax.random.randint(jax.random.fold_in(key, 5), (2,), 0, TOKEN_TOTAL)
    token_position = jnp.arange(TOKEN_TOTAL)
    spike_flag = jnp.any(token_position[None, :] == spike_locations[:, None], axis=0)
    spike_penalty = jnp.log(jax.random.uniform(jax.random.fold_in(key, 6), (HEAD_TOTAL,), jnp.float32, 0.65, 0.8))
    decay_amount = decay_amount + jnp.where(spike_flag[None, :], spike_penalty[:, None], 0.0)
    return decay_amount.astype(jnp.float32)


def draw_step_size(key, part):
    head_idx = jnp.arange(HEAD_TOTAL).astype(jnp.float32)
    head_rise = jnp.power(3.0, head_idx / (HEAD_TOTAL - 1))
    base_step = jnp.exp(jax.random.uniform(jax.random.fold_in(key, 1), (HEAD_TOTAL, TOKEN_TOTAL), jnp.float32, math.log(0.5), math.log(2.0)))
    return (base_step * head_rise[:, None]).astype(jnp.float32)


def draw_band_mask(key, part):
    blocks_dev = TOK_DEV // BLK
    block_idx = jnp.arange(QBLOCKS)[:, None]
    offset = jnp.arange(BAND)[None, :]
    target = block_idx - offset
    inside = (target >= 0) & (target // blocks_dev >= block_idx // blocks_dev - CYCLE)
    level_draw = jax.random.randint(jax.random.fold_in(key, 1), (QBLOCKS, 1), 15, 96)
    roll_draw = jax.random.randint(jax.random.fold_in(key, 2), (QBLOCKS, BAND), 0, 100)
    chosen = (roll_draw < level_draw) | (offset == 0)
    return jnp.where(inside & chosen, 1, 0).astype(jnp.int32)


def shard_levels(key, shape, split, low, high):
    factor_of, own = 1.0, jax.random.fold_in(key, 6)
    for axis_at, blocks in split:
        heights = jnp.exp(jax.random.uniform(jax.random.fold_in(own, axis_at), (blocks,), jnp.float32, low / len(split), high / len(split)))
        factor_of = factor_of * jnp.repeat(heights, shape[axis_at] // blocks).reshape([-1 if axis == axis_at else 1 for axis in range(len(shape))])
    return factor_of


def centred(key, extent, deviation, limit, shards=(), kind=jnp.bfloat16):
    gain = shard_levels(key, extent, shards, -0.22, 0.18) if shards else 1.0
    result = jax.random.normal(key, extent, jnp.float32) * deviation * gain
    return jnp.minimum(jnp.maximum(result, -limit), limit).astype(kind)


def setup_inputs(seed: int = 0) -> dict:
    arg_keys = jax.random.split(jax.random.key(seed), 8)
    query_rows = draw_query_rows(jax.random.fold_in(arg_keys[7], 71), 0)
    key_rows = draw_key_rows(jax.random.fold_in(arg_keys[7], 71), 0)
    value_rows = centred(arg_keys[2], (TOKEN_TOTAL, HEAD_TOTAL * HEAD_DIM), 1.0, 6.0, ((0, 64), (1, 4)))
    log_decay = draw_log_decay(jax.random.fold_in(arg_keys[7], 71), 0)
    step_size = draw_step_size(jax.random.fold_in(arg_keys[7], 71), 0)
    band_mask = draw_band_mask(jax.random.fold_in(arg_keys[7], 71), 0)
    cotangent = centred(arg_keys[6], (TOKEN_TOTAL, HEAD_TOTAL * HEAD_DIM), 1.0, 6.0, ((0, 64), (1, 4)))
    return dict(query_rows=query_rows, key_rows=key_rows, value_rows=value_rows, log_decay=log_decay, step_size=step_size, band_mask=band_mask, cotangent=cotangent)


def attention_block(query_blk, key_win, value_win, cot_blk, allowed):
    score_scale = HEAD_DIM ** (-0.5)
    query_f = query_blk.astype(jnp.float32)
    key_f = key_win.astype(jnp.float32)
    value_f = value_win.astype(jnp.float32)
    cot_f = cot_blk.astype(jnp.float32)
    scores = jnp.einsum('thd,uhd->htu', query_f, key_f) * score_scale
    scores = jnp.where(allowed[None, None, :], scores, -1e+30)
    row_peak = lax.optimization_barrier(jnp.max(scores, axis=-1, keepdims=True))
    exponent = jnp.exp(scores - row_peak)
    weights = exponent / lax.optimization_barrier(jnp.sum(exponent, axis=-1, keepdims=True))
    weights_bf = lax.optimization_barrier(weights.astype(jnp.bfloat16)).astype(jnp.float32)
    attended = jnp.einsum('htu,uhd->thd', weights_bf, value_f)
    inner_prod = jnp.einsum('thd,uhd->htu', cot_f, value_f)
    row_inner = lax.optimization_barrier(jnp.sum(cot_f * attended, axis=-1)).T[:, :, None]
    grad_scores = score_scale * weights * (inner_prod - row_inner)
    grad_scores = lax.optimization_barrier(grad_scores.astype(jnp.bfloat16)).astype(jnp.float32)
    grad_q = jnp.einsum('htu,uhd->thd', grad_scores, key_f)
    grad_k = jnp.einsum('htu,thd->uhd', grad_scores, query_f)
    grad_v = jnp.einsum('htu,thd->uhd', weights_bf, cot_f)
    return (attended, grad_q, grad_k, grad_v)

def attention_part(query_rows, key_rows, value_rows, band_mask, cotangent):
    feat_width = HEAD_TOTAL * HEAD_DIM
    padding = (BAND - 1) * BLK
    keys_padded = jnp.concatenate([jnp.zeros((padding, feat_width), jnp.bfloat16), key_rows], axis=0)
    values_padded = jnp.concatenate([jnp.zeros((padding, feat_width), jnp.bfloat16), value_rows], axis=0)
    query_blocks = query_rows.reshape(QBLOCKS, BLK, HEAD_TOTAL, HEAD_DIM)
    cot_blocks = cotangent.reshape(QBLOCKS, BLK, HEAD_TOTAL, HEAD_DIM)

    def advance(carried_acc, block_index):
        keys_acc, values_acc = carried_acc
        row_start = (block_index * BLK).astype(jnp.int32)
        key_win = lax.dynamic_slice_in_dim(keys_padded, row_start, BAND * BLK, 0).reshape(BAND * BLK, HEAD_TOTAL, HEAD_DIM)
        value_win = lax.dynamic_slice_in_dim(values_padded, row_start, BAND * BLK, 0).reshape(BAND * BLK, HEAD_TOTAL, HEAD_DIM)
        mask_row = lax.dynamic_index_in_dim(band_mask, block_index, 0, keepdims=False)
        allowed = jnp.repeat(mask_row[::-1] == 1, BLK)
        query_blk = lax.dynamic_index_in_dim(query_blocks, block_index, 0, keepdims=False)
        cot_blk = lax.dynamic_index_in_dim(cot_blocks, block_index, 0, keepdims=False)
        attended, grad_q, grad_k, grad_v = attention_block(query_blk, key_win, value_win, cot_blk, allowed)
        old_keys = lax.dynamic_slice_in_dim(keys_acc, row_start, BAND * BLK, 0)
        keys_acc = lax.dynamic_update_slice_in_dim(keys_acc, old_keys + grad_k.reshape(BAND * BLK, feat_width), row_start, 0)
        old_values = lax.dynamic_slice_in_dim(values_acc, row_start, BAND * BLK, 0)
        values_acc = lax.dynamic_update_slice_in_dim(values_acc, old_values + grad_v.reshape(BAND * BLK, feat_width), row_start, 0)
        return ((keys_acc, values_acc), (attended.reshape(BLK, feat_width), grad_q.reshape(BLK, feat_width)))
    start_acc = jnp.zeros((TOKEN_TOTAL + padding, feat_width), jnp.float32)
    (keys_acc, values_acc), (attended, grad_q) = lax.scan(advance, (start_acc, start_acc), jnp.arange(QBLOCKS, dtype=jnp.int32))
    return (attended.reshape(TOKEN_TOTAL, feat_width), grad_q.reshape(TOKEN_TOTAL, feat_width), keys_acc[padding:], values_acc[padding:])

def group_heads(rows):
    return rows.astype(jnp.float32).reshape(N_CTX, TOK_DEV, HEAD_TOTAL, HEAD_DIM).transpose(0, 2, 1, 3)

def rows_back(grouped):
    return grouped.transpose(0, 2, 1, 3).reshape(TOKEN_TOTAL, HEAD_TOTAL * HEAD_DIM)

def reference(query_rows, key_rows, value_rows, log_decay, step_size, band_mask, cotangent):
    highest = lax.Precision.HIGHEST
    score_scale = HEAD_DIM ** (-0.5)
    feat_width = HEAD_TOTAL * HEAD_DIM
    attended, att_dq, att_dk, att_dv = attention_part(query_rows, key_rows, value_rows, band_mask, cotangent)
    query_c = group_heads(query_rows)
    key_c = group_heads(key_rows)
    value_c = group_heads(value_rows)
    cot_c = group_heads(cotangent)
    decay_c = log_decay.reshape(HEAD_TOTAL, N_CTX, TOK_DEV).transpose(1, 0, 2)
    step_c = step_size.reshape(HEAD_TOTAL, N_CTX, TOK_DEV).transpose(1, 0, 2)
    prefix = jnp.cumsum(decay_c, axis=2)
    last_sum = prefix[:, :, -1]
    fade_total = jnp.exp(last_sum)
    carry_weight = jnp.exp(last_sum[:, :, None] - prefix) * step_c

    def summary(operand):
        weight_c, keys_in, values_in = operand
        return jnp.einsum('htn,htp->hnp', weight_c[:, :, None] * keys_in, values_in, precision=highest)
    local_state = lax.map(summary, (carry_weight, key_c, value_c))

    def chain_forward(running, operand):
        fade_one, local_one = operand
        return (fade_one[:, None, None] * running + local_one, running)
    zero_state = jnp.zeros((HEAD_TOTAL, HEAD_DIM, HEAD_DIM), jnp.float32)
    entry_state = lax.scan(chain_forward, zero_state, (fade_total, local_state))[1]
    token_position = jnp.arange(TOK_DEV)
    causal_mask = token_position[:, None] >= token_position[None, :]

    def group_work(operand):
        query_f, key_f, value_f, cot_f, prefix_one, step_one, entry_one = operand
        gap = jnp.where(causal_mask[None], prefix_one[:, :, None] - prefix_one[:, None, :], -jnp.inf)
        mixing = jnp.exp(gap) * step_one[:, None, :] * score_scale
        pair_prod = jnp.einsum('htn,hun->htu', query_f, key_f, precision=highest)
        paired = mixing * pair_prod
        decay_now = jnp.exp(prefix_one)[:, :, None]
        ssd_out = jnp.einsum('htu,hup->htp', paired, value_f, precision=highest)
        ssd_out = ssd_out + score_scale * decay_now * jnp.einsum('htn,hnp->htp', query_f, entry_one, precision=highest)
        root_mean = jnp.sqrt(lax.optimization_barrier(jnp.sum(ssd_out * ssd_out, axis=(0, 2))) / feat_width + 1e-05)[None, :, None]
        normed = ssd_out / root_mean
        cross_sum = (lax.optimization_barrier(jnp.sum(normed * cot_f, axis=(0, 2))) / feat_width)[None, :, None]
        d_ssd = (cot_f - normed * cross_sum) / root_mean
        own_back = score_scale * jnp.einsum('htn,htp->hnp', decay_now * query_f, d_ssd, precision=highest)
        inner_prod = jnp.einsum('htp,hup->htu', d_ssd, value_f, precision=highest)
        weighted = mixing * inner_prod
        ssd_dq = jnp.einsum('htu,hun->htn', weighted, key_f, precision=highest)
        ssd_dq = ssd_dq + score_scale * decay_now * jnp.einsum('hnp,htp->htn', entry_one, d_ssd, precision=highest)
        ssd_dk = jnp.einsum('htu,htn->hun', weighted, query_f, precision=highest)
        ssd_dv = jnp.einsum('htu,htp->hup', paired, d_ssd, precision=highest)
        return (normed, own_back, ssd_dq, ssd_dk, ssd_dv)
    normed, own_back, ssd_dq, ssd_dk, ssd_dv = lax.map(group_work, (query_c, key_c, value_c, cot_c, prefix, step_c, entry_state))

    def chain_backward(running, operand):
        fade_one, own_one = operand
        return (fade_one[:, None, None] * running + own_one, running)
    back_state = lax.scan(chain_backward, zero_state, (fade_total, own_back), reverse=True)[1]
    ssd_dk = ssd_dk + carry_weight[..., None] * jnp.einsum('chnp,chup->chun', back_state, value_c, precision=highest)
    ssd_dv = ssd_dv + carry_weight[..., None] * jnp.einsum('chnp,chun->chup', back_state, key_c, precision=highest)
    mixed_out = (attended + rows_back(normed)).astype(jnp.bfloat16)
    grad_queries = (att_dq + rows_back(ssd_dq)).astype(jnp.bfloat16)
    grad_keys = (att_dk + rows_back(ssd_dk)).astype(jnp.bfloat16)
    grad_values = (att_dv + rows_back(ssd_dv)).astype(jnp.bfloat16)
    return (mixed_out, grad_queries, grad_keys, grad_values)
```

```python
import functools

import jax
import jax.numpy as jnp
from jax import lax
from jax.experimental import pallas as pl
from jax.experimental.pallas import tpu as pltpu
from jax.sharding import PartitionSpec as P

MESH = pl.DeviceIdType.MESH
HIGHEST = lax.Precision.HIGHEST
F32 = jnp.float32
BF16 = jnp.bfloat16
D = 128
HH = 4
HW = HH * D
T2 = 256
W3 = 768
CHANNELS = 4096
SCALE = D ** (-0.5)
BIG = 1e30


def nn(a, b):
    return lax.dot_general(a, b, (((1,), (0,)), ((), ())), preferred_element_type=F32)


def nt(a, b):
    return lax.dot_general(a, b, (((1,), (1,)), ((), ())), preferred_element_type=F32)


def tn(a, b):
    return lax.dot_general(a, b, (((0,), (0,)), ((), ())), preferred_element_type=F32)


def kernel(
    nc, nx,
    q_ref, k_ref, v_ref, g_ref, ld_ref, st_ref, bm_ref,
    om_ref, oq_ref, ok_ref, ov_ref,
    kb, vb, qb, gb, ldb, stb, mk, f_out, f_in, l_out, l_in, e_out, e_in,
    o_in, o_out, b_out, b_in, xs, stat, rows, cols, bias, big,
    mix, mixt, pairt, ssd, dss, att, dq, dk, dv, outs,
    ssem, rsem, lsem,
):
    me = lax.axis_index("ctx")
    x = lax.axis_index("head")
    c = me // 2
    j = me % 2
    part = 512 // nc

    def dev(chip, core, xx):
        return (lax.rem(chip, nc) * 2 + core, xx)

    def order(n):
        half = (n + 1) // 2
        return nc // 2 + jnp.where(n % 2 == 0, half, -half)

    barrier = pltpu.get_barrier_semaphore()

    def greet(n, carry):
        pl.semaphore_signal(barrier, 1, device_id=dev(c + order(n), j, x), device_id_type=MESH)
        return carry

    lax.fori_loop(0, nc - 1, greet, 0)
    greeted = nc - 1
    for other in (dev(c + 1, 1 - j, x), dev(c + nc - 1, 1 - j, x), dev(c, 1 - j, x)):
        pl.semaphore_signal(barrier, 1, device_id=other, device_id_type=MESH)
        greeted += 1
    for step in range(1, nx):
        for core in range(2):
            pl.semaphore_signal(
                barrier, 1, device_id=dev(c, core, lax.rem(x + step, nx)), device_id_type=MESH
            )
            greeted += 1

    sends = []
    count = {"s": 0, "r": 0}

    def slots(kind, n):
        at = count[kind]
        count[kind] += n
        return at

    def remote(src, dst, recv, target):
        copy = pltpu.make_async_remote_copy(
            src_ref=src, dst_ref=dst, send_sem=ssem.at[slots("s", 1)], recv_sem=rsem.at[recv],
            device_id=target, device_id_type=MESH,
        )
        sends.append((copy, src))
        copy.start()

    def arrived(ref, recv):
        pltpu.make_async_copy(ref, ref, rsem.at[recv]).wait()

    mine = pl.ds(pl.multiple_of(j * HW, HW), HW)
    other_half = pl.ds(pl.multiple_of((1 - j) * HW, HW), HW)
    local = []
    for n, (src, dst, slot) in enumerate(
        ((k_ref, kb, 2), (v_ref, vb, 2), (q_ref, qb, 0), (g_ref, gb, 0))
    ):
        copy = pltpu.make_async_copy(src.at[:, mine], dst.at[slot, j], lsem.at[n])
        copy.start()
        local.append(copy)
    ldb[j] = ld_ref[...]
    stb[j] = st_ref[...]
    listed = bm_ref[...].astype(F32)
    mk[j] = jnp.concatenate(
        [jnp.broadcast_to(listed[:, n : n + 1], (1, D)) for n in range(5)]
        + [jnp.zeros((3, D), F32)],
        axis=0,
    )

    pl.semaphore_wait(barrier, greeted)

    mate = dev(c, 1 - j, x)
    small = slots("r", 3)
    remote(ldb.at[j], ldb.at[j], small, mate)
    remote(stb.at[j], stb.at[j], small + 1, mate)
    remote(mk.at[j], mk.at[j], small + 2, mate)
    swap = slots("r", 4)
    for n, (src, dst, slot) in enumerate(
        ((k_ref, kb, 2), (v_ref, vb, 2), (q_ref, qb, 0), (g_ref, gb, 0))
    ):
        remote(src.at[:, other_half], dst.at[slot, j], swap + n, mate)
    first = slots("r", 8)
    for n, (src, dst, step) in enumerate(
        ((k_ref, kb, 1), (q_ref, qb, nc - 1), (v_ref, vb, 1), (g_ref, gb, nc - 1))
    ):
        for core in range(2):
            remote(
                src.at[:, pl.ds(core * HW, HW)], dst.at[1, j], first + 2 * n + j,
                dev(c + step, core, x),
            )

    for n, ref in enumerate((ldb, stb, mk)):
        arrived(ref.at[1 - j], small + n)
    low = j == 0
    pair = []
    for ref in (ldb, stb):
        wide = jnp.concatenate([ref[0], ref[1]], axis=1)
        pair.append(jnp.where(low, wide[0:HH], wide[HH : 2 * HH]))
    decay, step_row = pair
    at_row = lax.broadcasted_iota(jnp.int32, (T2, T2), 0)
    at_col = lax.broadcasted_iota(jnp.int32, (T2, T2), 1)
    upper = (at_row <= at_col).astype(F32)
    prefix = lax.dot_general(
        jnp.concatenate([decay, decay], axis=0), upper, (((1,), (0,)), ((), ())),
        precision=HIGHEST, preferred_element_type=F32,
    )[0:HH]
    last = prefix[:, T2 - 1 : T2]
    carry_row = jnp.exp(last - prefix) * step_row
    packed = jnp.concatenate([prefix, step_row, carry_row, jnp.exp(prefix)], axis=0)
    rows[...] = packed
    cols[...] = jnp.transpose(packed)
    last_wide = jnp.broadcast_to(last, (HH, D))
    fade_tile = jnp.concatenate([last_wide, last_wide], axis=0)
    f_out[...] = fade_tile
    f_in[pl.ds(c, 1)] = fade_tile[None]

    a2a = []

    def exchange(src_of, dst_of):
        s_at, r_at = slots("s", 1), slots("r", 1)

        def one(n, carry):
            chip = lax.rem(c + order(n), nc)
            pltpu.make_async_remote_copy(
                src_ref=src_of(chip), dst_ref=dst_of(c), send_sem=ssem.at[s_at],
                recv_sem=rsem.at[r_at], device_id=(chip * 2 + j, x), device_id_type=MESH,
            ).start()
            return carry

        lax.fori_loop(0, nc - 1, one, 0)
        return s_at, r_at

    def own(chip):
        return pl.ds(pl.multiple_of(chip * part, part), part)

    f_sem = exchange(lambda chip: f_out, lambda sender: f_in.at[sender])

    for n in range(4):
        local[n].wait()
    arrived(kb.at[2, 1 - j], swap)
    arrived(vb.at[2, 1 - j], swap + 1)

    def head(ref, slot, h):
        return ref[slot, :, :, h * D : (h + 1) * D].reshape(T2, D)

    def band(ref, h):
        return ref[:, :, :, h * D : (h + 1) * D].reshape(W3, D)

    for h in range(HH):
        weighted = (cols[:, 8 + h : 9 + h] * head(kb, 2, h).astype(F32)).astype(BF16)
        l_out[h * D : (h + 1) * D, :] = tn(weighted, head(vb, 2, h)).astype(BF16)
    l_in[pl.ds(c, 1)] = l_out[own(c), :][None]
    l_sem = exchange(lambda chip: l_out.at[own(chip)], lambda sender: l_in.at[sender])

    blank = jnp.full((1, D), BIG, F32)
    for core in range(2):
        line = []
        for dist in (2, 1, 0):
            for core_k in range(2):
                off = 2 * dist + core - core_k
                line.append((1.0 - mk[core, off : off + 1, :]) * BIG if 0 <= off < 5 else blank)
        bias[core : core + 1, :] = jnp.concatenate(line, axis=1) * -1.0

    arrived(qb.at[0, 1 - j], swap + 2)
    arrived(gb.at[0, 1 - j], swap + 3)
    for h in range(HH):
        q, k, v = head(qb, 0, h), head(kb, 2, h), head(vb, 2, h)
        p_row, p_col = rows[h : h + 1, :], cols[:, h : h + 1]
        m = jnp.exp(jnp.where(at_row >= at_col, p_col - p_row, -BIG)) * (
            rows[4 + h : 5 + h, :] * SCALE
        )
        mix[h] = m
        ssd[h] = nn((m * nt(q, k)).astype(BF16), v)
        mt = jnp.exp(jnp.where(at_row <= at_col, p_row - p_col, -BIG)) * (
            cols[:, 4 + h : 5 + h] * SCALE
        )
        mixt[h] = mt
        pairt[h] = (mt * nt(k, q)).astype(BF16)

    second = slots("r", 8)
    for n, (buf, step) in enumerate(((kb, 1), (qb, nc - 1), (vb, 1), (gb, nc - 1))):
        far = 0 if step == 1 else 2
        for core in range(2):
            arrived(buf.at[1, core], first + 2 * n + core)
            remote(buf.at[1, core], buf.at[far, core], second + 2 * n + core, dev(c + step, j, x))

    def total(ref):
        return ref.at[pl.ds(0, nc - 1)]

    head_of = c * part // D
    arrived(total(f_in), f_sem[1])
    arrived(total(l_in), l_sem[1])

    def scan(src, dst, reverse):
        def one(n, run):
            chip = nc - 1 - n if reverse else n
            dst[pl.ds(chip, 1)] = run.astype(BF16)[None]
            fade = jnp.exp(f_in[pl.ds(chip, 1), pl.ds(head_of, 1), :][0])
            return fade * run + src[pl.ds(chip, 1)][0].astype(F32)

        lax.fori_loop(0, nc, one, jnp.zeros((part, D), F32), unroll=True)

    scan(l_in, e_out, False)
    e_sem = exchange(lambda chip: e_out.at[chip], lambda sender: e_in.at[own(sender)])
    e_in[own(c), :] = e_out[pl.ds(c, 1)][0]

    rest = e_in.at[pl.ds(0, 512 - part)]
    arrived(rest, e_sem[1])
    squares = jnp.zeros((T2, D), F32)
    inner = jnp.zeros((T2, D), F32)
    for h in range(HH):
        state = e_in[h * D : (h + 1) * D, :]
        y = ssd[h] + (SCALE * cols[:, 12 + h : 13 + h]) * nn(head(qb, 0, h), state)
        ssd[h] = y
        squares = squares + y * y
        inner = inner + y * head(gb, 0, h).astype(F32)
    ones = jnp.ones((8, D), F32)

    def across(a):
        return lax.dot_general(
            ones, a, (((1,), (1,)), ((), ())), precision=HIGHEST, preferred_element_type=F32
        )

    sums = jnp.concatenate([across(squares)[0:4], across(inner)[0:4]], axis=0)
    here = x * 2 + j
    xs[pl.ds(here, 1)] = sums[None]
    x_s, x_r = slots("s", 1), slots("r", 1)
    for step in range(nx):
        for core in range(2):
            if step == 0 and core == 0:
                continue
            pltpu.make_async_remote_copy(
                src_ref=xs.at[here], dst_ref=xs.at[here], send_sem=ssem.at[x_s],
                recv_sem=rsem.at[x_r],
                device_id=dev(c, (j + core) % 2, lax.rem(x + step, nx)), device_id_type=MESH,
            ).start()

    columns = []

    def query_side(h):
        q, g = head(qb, 0, h), head(gb, 0, h)
        k, v = band(kb, h), band(vb, h)
        s = nt(q, k) * SCALE
        s = (s.reshape(2, D, W3) + bias[0:2, :][:, None, :]).reshape(T2, W3)
        peak = jnp.max(s, axis=-1, keepdims=True)
        e = jnp.exp(s - peak)
        inv = 1.0 / jnp.sum(e, axis=-1, keepdims=True)
        w = e * inv
        a = nn(w.astype(BF16), v)
        att[h] = a
        row_inner = jnp.sum(g.astype(F32) * a, axis=-1, keepdims=True)
        gs = (SCALE * w * (nt(g, v) - row_inner)).astype(BF16)
        dq[h] = nn(gs, k)
        columns.append((peak, inv, row_inner))

    for core in range(2):
        arrived(kb.at[0, core], second + core)
        arrived(vb.at[0, core], second + 4 + core)
    query_side(0)
    query_side(1)

    arrived(xs.at[pl.ds(0, 2 * nx - 1)], x_r)
    both = xs[0]
    for n in range(1, 2 * nx):
        both = both + xs[n]
    inv_root = 1.0 / jnp.sqrt(both[0:4] / CHANNELS + 1e-05)
    cross = both[4:8] * inv_root / CHANNELS
    turned = jnp.transpose(jnp.concatenate([inv_root, inv_root * inv_root * cross], axis=0))
    root_col, slope_col = turned[:, 0:1], turned[:, 4:5]
    for h in range(HH):
        g = head(gb, 0, h).astype(F32)
        y = ssd[h]
        d = (g * root_col - y * slope_col).astype(BF16)
        dss[h] = d
        faded = (cols[:, 12 + h : 13 + h] * head(qb, 0, h).astype(F32)).astype(BF16)
        o_out[h * D : (h + 1) * D, :] = (SCALE * tn(faded, d)).astype(BF16)
        ssd[h] = y * root_col
    o_in[pl.ds(c, 1)] = o_out[own(c), :][None]
    o_sem = exchange(lambda chip: o_out.at[own(chip)], lambda sender: o_in.at[sender])

    query_side(2)
    query_side(3)

    lane = lax.broadcasted_iota(jnp.int32, (T2, D), 1)
    grid = jnp.zeros((T2, D), F32)
    for kind in range(3):
        for h in range(HH):
            grid = jnp.where(lane == kind * HH + h, columns[h][kind], grid)
    stat[0, 0:16, :] = jnp.transpose(grid)[0:16]
    stat[0, 16:24, :] = jnp.concatenate([mk[0], mk[1]], axis=1)
    stat_r = slots("r", 2)
    for dist in (1, 2):
        remote(stat.at[0], stat.at[dist], stat_r + dist - 1, dev(c + nc - dist, j, x))

    out_sends = []
    out_local = []
    out_r = slots("r", 4)

    def emit(n, ref):
        copy = pltpu.make_async_copy(outs.at[n, j], ref.at[:, mine], lsem.at[4 + n])
        copy.start()
        out_local.append(copy)
        far = pltpu.make_async_remote_copy(
            src_ref=outs.at[n, 1 - j], dst_ref=ref.at[:, mine], send_sem=ssem.at[slots("s", 1)],
            recv_sem=rsem.at[out_r + n], device_id=mate, device_id_type=MESH,
        )
        far.start()
        out_sends.append(far)

    def put(n, h, value):
        outs[n, :, :, h * D : (h + 1) * D] = value.astype(BF16).reshape(2, D, D)

    for h in range(HH):
        q, k, v, d = head(qb, 0, h), head(kb, 2, h), head(vb, 2, h), dss[h]
        state = e_in[h * D : (h + 1) * D, :]
        put(0, h, att[h] + ssd[h])
        grad = nn((mix[h] * nt(d, v)).astype(BF16), k)
        grad = grad + (SCALE * cols[:, 12 + h : 13 + h]) * nt(d, state)
        put(1, h, dq[h] + grad)
        dk[h] = nn((mixt[h] * nt(v, d)).astype(BF16), q)
        dv[h] = nn(pairt[h], d)
    emit(0, om_ref)
    emit(1, oq_ref)

    arrived(total(o_in), o_sem[1])
    scan(o_in, b_out, True)
    b_sem = exchange(lambda chip: b_out.at[chip], lambda sender: b_in.at[own(sender)])
    b_in[own(c), :] = b_out[pl.ds(c, 1)][0]

    for dist in (1, 2):
        arrived(stat.at[dist], stat_r + dist - 1)
    for core in range(2):
        arrived(qb.at[2, core], second + 2 + core)
        arrived(gb.at[2, core], second + 6 + core)
    for core_k in range(2):
        line = []
        for dist in range(3):
            here_ok = c + dist < nc
            for core in range(2):
                off = 2 * dist + core - core_k
                if 0 <= off < 5:
                    listed = stat[dist, 16 + off : 17 + off, core * D : (core + 1) * D]
                    line.append(jnp.where(here_ok, (1.0 - listed) * BIG, BIG))
                else:
                    line.append(blank)
        big[core_k : core_k + 1, :] = jnp.concatenate(line, axis=1)
    for h in range(HH):
        q, g = band(qb, h), band(gb, h)
        k, v = head(kb, 2, h), head(vb, 2, h)
        peak, inv, row_inner = [
            jnp.concatenate([stat[n, kind * HH + h : kind * HH + h + 1, :] for n in range(3)], axis=1)
            for kind in range(3)
        ]
        shift = peak + big[0:2, :]
        s = nt(k, q) * SCALE
        w = jnp.exp((s.reshape(2, D, W3) - shift[:, None, :]).reshape(T2, W3)) * inv
        dv[h] = dv[h] + nn(w.astype(BF16), g)
        gs = (SCALE * w * (nt(v, g) - row_inner)).astype(BF16)
        dk[h] = dk[h] + nn(gs, q)

    arrived(b_in.at[pl.ds(0, 512 - part)], b_sem[1])
    for h in range(HH):
        state = b_in[h * D : (h + 1) * D, :]
        weight = cols[:, 8 + h : 9 + h]
        put(2, h, dk[h] + weight * nt(head(vb, 2, h), state))
        put(3, h, dv[h] + weight * nn(head(kb, 2, h), state))
    emit(2, ok_ref)
    emit(3, ov_ref)

    for copy, _ in sends:
        copy.wait_send()
    pltpu.make_async_copy(total(f_in), total(f_in), ssem.at[f_sem[0]]).wait()
    for ref, sem in ((l_in, l_sem), (e_out, e_sem), (o_in, o_sem), (b_out, b_sem)):
        pltpu.make_async_copy(total(ref), total(ref), ssem.at[sem[0]]).wait()
    rest_x = xs.at[pl.ds(0, 2 * nx - 1)]
    pltpu.make_async_copy(rest_x, rest_x, ssem.at[x_s]).wait()
    for copy in out_local:
        copy.wait()
    for copy in out_sends:
        copy.wait()


def solution(mesh):
    nc = mesh.shape["ctx"] // 2
    nx = mesh.shape["head"]
    part = 512 // nc

    def body(query_rows, key_rows, value_rows, log_decay, step_size, band_mask, cotangent):
        tok, width = query_rows.shape
        out = jax.ShapeDtypeStruct((tok, width), BF16)
        hbm = pl.BlockSpec(memory_space=pl.ANY)
        vmem = pl.BlockSpec(memory_space=pltpu.VMEM)
        band = pltpu.VMEM((3, 2, D, HW), BF16)
        tile2 = pltpu.VMEM((2, 8, D), F32)
        share = pltpu.VMEM((nc, part, D), BF16)
        whole = pltpu.VMEM((HW, D), BF16)
        per_head = pltpu.VMEM((HH, T2, D), F32)
        square = pltpu.VMEM((HH, T2, T2), F32)
        return pl.pallas_call(
            functools.partial(kernel, nc, nx),
            name="mixer",
            out_shape=(out,) * 4,
            in_specs=[hbm] * 4 + [vmem] * 3,
            out_specs=(hbm,) * 4,
            scratch_shapes=[
                band, band, band, band, tile2, tile2, tile2,
                pltpu.VMEM((8, D), F32), pltpu.VMEM((nc, 8, D), F32),
                whole, share, share, whole,
                share, whole, share, whole,
                pltpu.VMEM((2 * nx, 8, T2), F32), pltpu.VMEM((3, 24, T2), F32),
                pltpu.VMEM((16, T2), F32), pltpu.VMEM((T2, 16), F32),
                pltpu.VMEM((8, W3), F32), pltpu.VMEM((8, W3), F32),
                square, square, pltpu.VMEM((HH, T2, T2), BF16),
                per_head, pltpu.VMEM((HH, T2, D), BF16),
                per_head, per_head, per_head, per_head,
                pltpu.VMEM((4, 2, D, HW), BF16),
                pltpu.SemaphoreType.DMA((48,)), pltpu.SemaphoreType.DMA((48,)),
                pltpu.SemaphoreType.DMA((8,)),
            ],
            compiler_params=pltpu.CompilerParams(
                collective_id=0, has_side_effects=True, vmem_limit_bytes=48 << 20
            ),
        )(query_rows, key_rows, value_rows, cotangent, log_decay, step_size, band_mask)

    return jax.shard_map(
        body,
        mesh=mesh,
        in_specs=(
            P("ctx", "head"),
            P("ctx", "head"),
            P("ctx", "head"),
            P("head", "ctx"),
            P("head", "ctx"),
            P("ctx", None),
            P("ctx", "head"),
        ),
        out_specs=(P("ctx", "head"), P("ctx", "head"), P("ctx", "head"), P("ctx", "head")),
        check_vma=False,
    )
```

```python
import functools

import jax
import jax.numpy as jnp
from jax import lax
from jax.experimental import pallas as pl
from jax.experimental.pallas import tpu as pltpu
from jax.sharding import PartitionSpec as P

MESH = pl.DeviceIdType.MESH
HIGHEST = lax.Precision.HIGHEST
F32 = jnp.float32
BF16 = jnp.bfloat16
D = 128
HH = 4
HW = HH * D
T2 = 256
W3 = 768
CHANNELS = 4096
SCALE = D ** (-0.5)
BIG = 1e30
PLAN = {
    "p": ("k1a", "q1a"),
    "l": ("k1b", "q1b", "v1a", "g1a", "intra"),
    "e": ("v1b", "g1b", "k2a", "q2a", "k2b", "q2b"),
    "x": ("v2a", "g2a"),
    "o": ("v2b", "g2b", "soft", "ssd"),
    "b": ("query", "early", "late"),
}


def nn(a, b):
    return lax.dot_general(a, b, (((1,), (0,)), ((), ())), preferred_element_type=F32)


def nt(a, b):
    return lax.dot_general(a, b, (((1,), (1,)), ((), ())), preferred_element_type=F32)


def tn(a, b):
    return lax.dot_general(a, b, (((0,), (0,)), ((), ())), preferred_element_type=F32)


def kernel(
    nc, nx,
    q_ref, k_ref, v_ref, g_ref, ld_ref, st_ref, bm_ref,
    om_ref, oq_ref, ok_ref, ov_ref,
    kb, vb, qb, gb, kx, vx, ldb, stb, mk, bmv, part_out, part_in, f_in, l_out, l_in, e_out, e_in,
    o_in, o_out, b_out, b_in, xs, stat, rows, cols, bias, big,
    mix, mixt, pairt, qt, ssd, dss, wq, wk, dq, dk, dv, outs,
    ssem, rsem, lsem,
):
    me = lax.axis_index("ctx")
    x = lax.axis_index("head")
    c = me // 2
    j = me % 2
    part = 512 // nc

    def dev(chip, core, xx):
        return (lax.rem(chip, nc) * 2 + core, xx)

    def order(n):
        half = (n + 1) // 2
        return nc // 2 + jnp.where(n % 2 == 0, half, -half)

    barrier = pltpu.get_barrier_semaphore()

    def greet(n, carry):
        pl.semaphore_signal(barrier, 1, device_id=dev(c + order(n), j, x), device_id_type=MESH)
        return carry

    lax.fori_loop(0, nc - 1, greet, 0)
    greeted = nc - 1
    for other in (dev(c + 1, 1 - j, x), dev(c + nc - 1, 1 - j, x), dev(c, 1 - j, x)):
        pl.semaphore_signal(barrier, 1, device_id=other, device_id_type=MESH)
        greeted += 1
    for step in range(1, nx):
        for core in range(2):
            pl.semaphore_signal(
                barrier, 1, device_id=dev(c, core, lax.rem(x + step, nx)), device_id_type=MESH
            )
            greeted += 1

    sends = []
    count = {"s": 0, "r": 0}

    def slots(kind, n):
        at = count[kind]
        count[kind] += n
        return at

    def remote(src, dst, recv, target):
        copy = pltpu.make_async_remote_copy(
            src_ref=src, dst_ref=dst, send_sem=ssem.at[slots("s", 1)], recv_sem=rsem.at[recv],
            device_id=target, device_id_type=MESH,
        )
        sends.append((copy, src))
        copy.start()

    def arrived(ref, recv):
        pltpu.make_async_copy(ref, ref, rsem.at[recv]).wait()

    mine = pl.ds(pl.multiple_of(j * HW, HW), HW)
    other_half = pl.ds(pl.multiple_of((1 - j) * HW, HW), HW)
    local = []
    for n, (src, dst) in enumerate(
        (
            (ld_ref, ldb.at[j]), (st_ref, stb.at[j]), (bm_ref, bmv),
            (k_ref.at[:, mine], kb.at[2, j]), (v_ref.at[:, mine], vb.at[2, j]),
            (k_ref.at[:, other_half], kx), (v_ref.at[:, other_half], vx),
            (q_ref.at[:, mine], qb.at[0, j]), (g_ref.at[:, mine], gb.at[0, j]),
        )
    ):
        copy = pltpu.make_async_copy(src, dst, lsem.at[n])
        copy.start()
        local.append(copy)
    low = j == 0
    at_row = lax.broadcasted_iota(jnp.int32, (T2, T2), 0)
    at_col = lax.broadcasted_iota(jnp.int32, (T2, T2), 1)
    upper = (at_row <= at_col).astype(F32)
    for copy in local[0:3]:
        copy.wait()
    listed = bmv[...].astype(F32)
    mk[j] = jnp.concatenate(
        [jnp.broadcast_to(listed[:, n : n + 1], (1, D)) for n in range(5)]
        + [jnp.zeros((3, D), F32)],
        axis=0,
    )
    own_prefix = lax.dot_general(
        ldb[j], upper[0:D, 0:D], (((1,), (0,)), ((), ())),
        precision=HIGHEST, preferred_element_type=F32,
    )
    own_carry = jnp.transpose(jnp.exp(own_prefix[:, D - 1 : D] - own_prefix) * stb[j])
    carry_mine = jnp.where(low, own_carry[:, 0:HH], own_carry[:, HH : 2 * HH])
    carry_mate = jnp.where(low, own_carry[:, HH : 2 * HH], own_carry[:, 0:HH])
    for copy in local[3:7]:
        copy.wait()
    for h in range(HH):
        cut = slice(h * D, (h + 1) * D)
        part_out[cut, :] = tn(
            (carry_mate[:, h : h + 1] * kx[:, cut].astype(F32)).astype(BF16), vx[:, cut]
        )
        part_in[j, cut, :] = tn(
            (carry_mine[:, h : h + 1] * kb[2, j, :, cut].astype(F32)).astype(BF16),
            vb[2, j, :, cut],
        )

    pl.semaphore_wait(barrier, greeted)

    mate = dev(c, 1 - j, x)
    small = slots("r", 4)
    remote(ldb.at[j], ldb.at[j], small, mate)
    remote(stb.at[j], stb.at[j], small + 1, mate)
    remote(part_out, part_in.at[j], small + 2, mate)
    remote(mk.at[j], mk.at[j], small + 3, mate)
    swap = slots("r", 4)

    def swap_send(n, src, dst, slot):
        remote(src, dst.at[slot, j], swap + n, mate)

    swap_send(0, kx, kb, 2)
    swap_send(1, vx, vb, 2)
    swap_send(2, q_ref.at[:, other_half], qb, 0)
    swap_send(3, g_ref.at[:, other_half], gb, 0)

    first = slots("r", 16)
    second = slots("r", 16)
    ways = {
        "k": (0, k_ref, kb, 0, 1), "q": (1, q_ref, qb, 2, nc - 1),
        "v": (2, v_ref, vb, 0, 1), "g": (3, g_ref, gb, 2, nc - 1),
    }

    def half(name):
        at = 4 * ways[name[0]][0] + 2 * (name[2] == "b")
        return pl.ds(64 * (name[2] == "b"), 64), first + at, second + at

    def own_on(name):
        _, src, dst, _, step = ways[name[0]]
        lines, near, _ = half(name)
        for core in range(2):
            remote(
                src.at[lines, pl.ds(core * HW, HW)], dst.at[1, j, lines], near + j,
                dev(c + step, core, x),
            )

    def hand_on(name):
        _, _, buf, far, step = ways[name[0]]
        lines, near, later = half(name)
        for core in range(2):
            arrived(buf.at[1, core, lines], near + core)
            remote(
                buf.at[1, core, lines], buf.at[far, core, lines], later + core, dev(c + step, j, x)
            )

    def landed(name):
        _, _, buf, far, _ = ways[name]
        for end in "ab":
            lines, _, later = half(name + "2" + end)
            for core in range(2):
                arrived(buf.at[far, core, lines], later + core)

    acts = {}

    def during(window):
        for item in PLAN[window]:
            if item in acts:
                acts[item]()
            elif item[1] == "1":
                own_on(item)
            else:
                hand_on(item)

    during("p")

    arrived(ldb.at[1 - j], small)
    arrived(stb.at[1 - j], small + 1)
    pair = []
    for ref in (ldb, stb):
        wide = jnp.concatenate([ref[0], ref[1]], axis=1)
        pair.append(jnp.where(low, wide[0:HH], wide[HH : 2 * HH]))
    decay, step_row = pair
    last_wide = jnp.broadcast_to(jnp.sum(decay, axis=1, keepdims=True), (HH, D))
    f_in[pl.ds(c, 1)] = jnp.concatenate([last_wide, last_wide], axis=0)[None]

    def exchange(src_of, dst_of):
        s_at, r_at = slots("s", 1), slots("r", 1)

        def one(n, carry):
            chip = lax.rem(c + order(n), nc)
            pltpu.make_async_remote_copy(
                src_ref=src_of(chip), dst_ref=dst_of(c), send_sem=ssem.at[s_at],
                recv_sem=rsem.at[r_at], device_id=(chip * 2 + j, x), device_id_type=MESH,
            ).start()
            return carry

        lax.fori_loop(0, nc - 1, one, 0)
        return s_at, r_at

    def own(chip):
        return pl.ds(pl.multiple_of(chip * part, part), part)

    def head(ref, slot, h):
        return ref[slot, :, :, h * D : (h + 1) * D].reshape(T2, D)

    def band(ref, h):
        return ref[:, :, :, h * D : (h + 1) * D].reshape(W3, D)

    fade_late = jnp.exp(jnp.sum(decay[:, D : 2 * D], axis=1, keepdims=True))
    arrived(part_in.at[1 - j], small + 2)
    for h in range(HH):
        cut = slice(h * D, (h + 1) * D)
        l_out[cut, :] = (fade_late[h : h + 1, :] * part_in[0, cut, :] + part_in[1, cut, :]).astype(BF16)
    l_sem = exchange(lambda chip: l_out.at[own(chip)], lambda sender: l_in.at[sender])
    l_in[pl.ds(c, 1)] = l_out[own(c), :][None]

    f_sem = exchange(lambda chip: f_in.at[c], lambda sender: f_in.at[sender])

    blank = jnp.full((1, D), BIG, F32)

    def intra():
        prefix = lax.dot_general(
            jnp.concatenate([decay, decay], axis=0), upper, (((1,), (0,)), ((), ())),
            precision=HIGHEST, preferred_element_type=F32,
        )[0:HH]
        last = prefix[:, T2 - 1 : T2]
        carry_row = jnp.exp(last - prefix) * step_row
        packed = jnp.concatenate([prefix, step_row, carry_row, jnp.exp(prefix)], axis=0)
        rows[...] = packed
        cols[...] = jnp.transpose(packed)

        arrived(mk.at[1 - j], small + 3)

        for core in range(2):
            line = []
            for dist in (2, 1, 0):
                for core_k in range(2):
                    off = 2 * dist + core - core_k
                    line.append((1.0 - mk[core, off : off + 1, :]) * BIG if 0 <= off < 5 else blank)
            bias[core : core + 1, :] = jnp.concatenate(line, axis=1) * -1.0

        for copy in local[7:9]:
            copy.wait()
        arrived(kb.at[2, 1 - j], swap)
        arrived(vb.at[2, 1 - j], swap + 1)
        arrived(qb.at[0, 1 - j], swap + 2)
        arrived(gb.at[0, 1 - j], swap + 3)
        for h in range(HH):
            q, k, v = head(qb, 0, h), head(kb, 2, h), head(vb, 2, h)
            p_row, p_col = rows[h : h + 1, :], cols[:, h : h + 1]
            m = jnp.exp(jnp.where(at_row >= at_col, p_col - p_row, -BIG)) * (
                rows[4 + h : 5 + h, :] * SCALE
            )
            mix[h] = m
            ssd[h] = nn((m * nt(q, k)).astype(BF16), v)
            mt = jnp.exp(jnp.where(at_row <= at_col, p_row - p_col, -BIG)) * (
                cols[:, 4 + h : 5 + h] * SCALE
            )
            mixt[h] = mt
            pairt[h] = (mt * nt(k, q)).astype(BF16)
            qt[h] = jnp.transpose(cols[:, 12 + h : 13 + h] * q.astype(F32)).astype(BF16)

    acts["intra"] = intra
    during("l")

    def total(ref):
        return ref.at[pl.ds(0, nc - 1)]

    head_of = c * part // D
    arrived(total(f_in), f_sem[1])
    arrived(total(l_in), l_sem[1])

    def scan(src, dst, reverse):
        def one(n, run):
            chip = nc - 1 - n if reverse else n
            dst[pl.ds(chip, 1)] = run.astype(BF16)[None]
            fade = jnp.exp(f_in[pl.ds(chip, 1), pl.ds(head_of, 1), :][0])
            return fade * run + src[pl.ds(chip, 1)][0].astype(F32)

        lax.fori_loop(0, nc, one, jnp.zeros((part, D), F32), unroll=True)

    scan(l_in, e_out, False)
    e_sem = exchange(lambda chip: e_out.at[chip], lambda sender: e_in.at[own(sender)])
    e_in[own(c), :] = e_out[pl.ds(c, 1)][0]

    during("e")

    rest = e_in.at[pl.ds(0, 512 - part)]
    arrived(rest, e_sem[1])
    squares = jnp.zeros((T2, D), F32)
    inner = jnp.zeros((T2, D), F32)
    for h in range(HH):
        state = e_in[h * D : (h + 1) * D, :]
        y = ssd[h] + (SCALE * cols[:, 12 + h : 13 + h]) * nn(head(qb, 0, h), state)
        ssd[h] = y
        squares = squares + y * y
        inner = inner + y * head(gb, 0, h).astype(F32)
    ones = jnp.ones((8, D), BF16)

    def across(a):
        head_part = a.astype(BF16)
        return nt(ones, head_part) + nt(ones, (a - head_part.astype(F32)).astype(BF16))

    sums = jnp.concatenate([across(squares)[0:4], across(inner)[0:4]], axis=0)
    here = x * 2 + j
    xs[pl.ds(here, 1)] = sums[None]
    x_s, x_r = slots("s", 1), slots("r", 1)
    for step in range(nx):
        for core in range(2):
            if step == 0 and core == 0:
                continue
            pltpu.make_async_remote_copy(
                src_ref=xs.at[here], dst_ref=xs.at[here], send_sem=ssem.at[x_s],
                recv_sem=rsem.at[x_r],
                device_id=dev(c, (j + core) % 2, lax.rem(x + step, nx)), device_id_type=MESH,
            ).start()

    columns = []

    def turned_rows(kinds):
        lane = lax.broadcasted_iota(jnp.int32, (T2, D), 1)
        grid = jnp.zeros((T2, D), F32)
        for n, column in enumerate(kinds):
            grid = jnp.where(lane == n, column, grid)
        return jnp.transpose(grid)[0:8]

    def send_stat(lines, at):
        for dist in (1, 2):
            remote(
                stat.at[0, lines], stat.at[dist, lines], at + dist - 1, dev(c + nc - dist, j, x)
            )

    stat_r = slots("r", 4)

    def soft():
        landed("k")
        for h in range(HH):
            s = nt(head(qb, 0, h), band(kb, h)) * SCALE
            s = (s.reshape(2, D, W3) + bias[0:2, :][:, None, :]).reshape(T2, W3)
            peak = jnp.max(s, axis=-1, keepdims=True)
            e = jnp.exp(s - peak)
            inv = 1.0 / jnp.sum(e, axis=-1, keepdims=True)
            wq[h] = e * inv
            columns.append((peak, inv))
        stat[0, 0:8, :] = turned_rows([p for p, _ in columns] + [i for _, i in columns])
        stat[0, 8:16, :] = jnp.concatenate([mk[0], mk[1]], axis=1)
        send_stat(pl.ds(0, 16), stat_r)

    acts["soft"] = soft
    during("x")

    arrived(xs.at[pl.ds(0, 2 * nx - 1)], x_r)
    both = xs[0]
    for n in range(1, 2 * nx):
        both = both + xs[n]
    inv_root = 1.0 / jnp.sqrt(both[0:4] / CHANNELS + 1e-05)
    cross = both[4:8] * inv_root / CHANNELS
    turned = jnp.transpose(jnp.concatenate([inv_root, inv_root * inv_root * cross], axis=0))
    root_col, slope_col = turned[:, 0:1], turned[:, 4:5]
    for h in range(HH):
        g = head(gb, 0, h).astype(F32)
        y = ssd[h]
        d = (g * root_col - y * slope_col).astype(BF16)
        dss[h] = d
        o_out[h * D : (h + 1) * D, :] = (SCALE * nn(qt[h], d)).astype(BF16)
    o_in[pl.ds(c, 1)] = o_out[own(c), :][None]
    o_sem = exchange(lambda chip: o_out.at[own(chip)], lambda sender: o_in.at[sender])

    out_sends = []
    out_local = []
    out_r = slots("r", 4)

    def emit(n, ref):
        copy = pltpu.make_async_copy(outs.at[n, j], ref.at[:, mine], lsem.at[9 + n])
        copy.start()
        out_local.append(copy)
        far = pltpu.make_async_remote_copy(
            src_ref=outs.at[n, 1 - j], dst_ref=ref.at[:, mine], send_sem=ssem.at[slots("s", 1)],
            recv_sem=rsem.at[out_r + n], device_id=mate, device_id_type=MESH,
        )
        far.start()
        out_sends.append(far)

    def put(n, h, value):
        outs[n, :, :, h * D : (h + 1) * D] = value.astype(BF16).reshape(2, D, D)

    def ssd_grads():
        for h in range(HH):
            q, k, v, d = head(qb, 0, h), head(kb, 2, h), head(vb, 2, h), dss[h]
            state = e_in[h * D : (h + 1) * D, :]
            grad = nn((mix[h] * nt(d, v)).astype(BF16), k)
            grad = grad + (SCALE * cols[:, 12 + h : 13 + h]) * nt(d, state)
            dq[h] = grad
            dk[h] = nn((mixt[h] * nt(v, d)).astype(BF16), q)
            dv[h] = nn(pairt[h], d)

    acts["ssd"] = ssd_grads
    during("o")

    arrived(total(o_in), o_sem[1])
    scan(o_in, b_out, True)
    b_sem = exchange(lambda chip: b_out.at[chip], lambda sender: b_in.at[own(sender)])
    b_in[own(c), :] = b_out[pl.ds(c, 1)][0]

    def query():
        landed("v")
        inners = []
        for h in range(HH):
            g, k, v, w = head(gb, 0, h), band(kb, h), band(vb, h), wq[h]
            a = nn(w.astype(BF16), v)
            row_inner = jnp.sum(g.astype(F32) * a, axis=-1, keepdims=True)
            inners.append(row_inner)
            put(0, h, a + ssd[h] * root_col)
            gs = (SCALE * w * (nt(g, v) - row_inner)).astype(BF16)
            put(1, h, nn(gs, k) + dq[h])
        stat[0, 16:24, :] = turned_rows(inners)
        send_stat(pl.ds(16, 8), stat_r + 2)
        emit(0, om_ref)
        emit(1, oq_ref)

    def early():
        for dist in (1, 2):
            arrived(stat.at[dist, pl.ds(0, 16)], stat_r + dist - 1)
        landed("q")
        for core_k in range(2):
            line = []
            for dist in range(3):
                here_ok = c + dist < nc
                for core in range(2):
                    off = 2 * dist + core - core_k
                    if 0 <= off < 5:
                        listed = stat[dist, 8 + off : 9 + off, core * D : (core + 1) * D]
                        line.append(jnp.where(here_ok, (1.0 - listed) * BIG, BIG))
                    else:
                        line.append(blank)
            big[core_k : core_k + 1, :] = jnp.concatenate(line, axis=1)
        landed("g")
        for h in range(HH):
            q, g, k = band(qb, h), band(gb, h), head(kb, 2, h)
            peak, inv = [
                jnp.concatenate([stat[n, at : at + 1, :] for n in range(3)], axis=1)
                for at in (h, HH + h)
            ]
            shift = peak + big[0:2, :]
            s = nt(k, q) * SCALE
            w = jnp.exp((s.reshape(2, D, W3) - shift[:, None, :]).reshape(T2, W3)) * inv
            dv[h] = dv[h] + nn(w.astype(BF16), g)
            wk[h] = w

    def late():
        for dist in (1, 2):
            arrived(stat.at[dist, pl.ds(16, 8)], stat_r + 1 + dist)
        for h in range(HH):
            row_inner = jnp.concatenate([stat[n, 16 + h : 17 + h, :] for n in range(3)], axis=1)
            gs = (SCALE * wk[h] * (nt(head(vb, 2, h), band(gb, h)) - row_inner)).astype(BF16)
            dk[h] = dk[h] + nn(gs, band(qb, h))

    acts["query"], acts["early"], acts["late"] = query, early, late
    during("b")

    arrived(b_in.at[pl.ds(0, 512 - part)], b_sem[1])
    for h in range(HH):
        state = b_in[h * D : (h + 1) * D, :]
        weight = cols[:, 8 + h : 9 + h]
        put(2, h, dk[h] + weight * nt(head(vb, 2, h), state))
    emit(2, ok_ref)
    for h in range(HH):
        state = b_in[h * D : (h + 1) * D, :]
        weight = cols[:, 8 + h : 9 + h]
        put(3, h, dv[h] + weight * nn(head(kb, 2, h), state))
    emit(3, ov_ref)

    for copy, _ in sends:
        copy.wait_send()
    pltpu.make_async_copy(total(f_in), total(f_in), ssem.at[f_sem[0]]).wait()
    for ref, sem in ((l_in, l_sem), (e_out, e_sem), (o_in, o_sem), (b_out, b_sem)):
        pltpu.make_async_copy(total(ref), total(ref), ssem.at[sem[0]]).wait()
    rest_x = xs.at[pl.ds(0, 2 * nx - 1)]
    pltpu.make_async_copy(rest_x, rest_x, ssem.at[x_s]).wait()
    for copy in out_local:
        copy.wait()
    for copy in out_sends:
        copy.wait()


def store(a, b, c, d, ra, rb, rc, rd):
    for src, dst in ((a, ra), (b, rb), (c, rc), (d, rd)):
        dst[...] = src[...]


def solution(mesh):
    nc = mesh.shape["ctx"] // 2
    nx = mesh.shape["head"]
    part = 512 // nc

    def body(query_rows, key_rows, value_rows, log_decay, step_size, band_mask, cotangent):
        tok, width = query_rows.shape
        out = jax.ShapeDtypeStruct((tok, width), BF16)
        hbm = pl.BlockSpec(memory_space=pltpu.HBM)
        band = pltpu.VMEM((3, 2, D, HW), BF16)
        tile2 = pltpu.VMEM((2, 8, D), F32)
        share = pltpu.VMEM((nc, part, D), BF16)
        whole = pltpu.VMEM((HW, D), BF16)
        per_head = pltpu.VMEM((HH, T2, D), F32)
        square = pltpu.VMEM((HH, T2, T2), F32)
        results = pl.pallas_call(
            functools.partial(kernel, nc, nx),
            name="mixer",
            out_shape=(out,) * 4,
            in_specs=[hbm] * 7,
            out_specs=(pl.BlockSpec(memory_space=pl.ANY),) * 4,
            scratch_shapes=[
                band, band, band, band, pltpu.VMEM((D, HW), BF16), pltpu.VMEM((D, HW), BF16),
                tile2, tile2, tile2, pltpu.VMEM((1, 5), jnp.int32),
                pltpu.VMEM((HW, D), F32), pltpu.VMEM((2, HW, D), F32), pltpu.VMEM((nc, 8, D), F32),
                whole, share, share, whole,
                share, whole, share, whole,
                pltpu.VMEM((2 * nx, 8, T2), F32), pltpu.VMEM((3, 24, T2), F32),
                pltpu.VMEM((16, T2), F32), pltpu.VMEM((T2, 16), F32),
                pltpu.VMEM((8, W3), F32), pltpu.VMEM((8, W3), F32),
                square, square, pltpu.VMEM((HH, T2, T2), BF16), pltpu.VMEM((HH, D, T2), BF16),
                per_head, pltpu.VMEM((HH, T2, D), BF16),
                pltpu.VMEM((HH, T2, W3), F32), pltpu.VMEM((HH, T2, W3), F32),
                per_head, per_head, per_head,
                pltpu.VMEM((4, 2, D, HW), BF16),
                pltpu.SemaphoreType.DMA((80,)), pltpu.SemaphoreType.DMA((80,)),
                pltpu.SemaphoreType.DMA((16,)),
            ],
            compiler_params=pltpu.CompilerParams(
                collective_id=0, has_side_effects=True, vmem_limit_bytes=56 << 20
            ),
        )(query_rows, key_rows, value_rows, cotangent, log_decay, step_size, band_mask)
        return pl.pallas_call(
            store,
            name="store",
            out_shape=(out,) * 4,
            grid=(2,),
            in_specs=[pl.BlockSpec((tok // 2, width), lambda n: (n, 0))] * 4,
            out_specs=(pl.BlockSpec((tok // 2, width), lambda n: (n, 0)),) * 4,
        )(*results)

    return jax.shard_map(
        body,
        mesh=mesh,
        in_specs=(
            P("ctx", "head"),
            P("ctx", "head"),
            P("ctx", "head"),
            P("head", "ctx"),
            P("head", "ctx"),
            P("ctx", None),
            P("ctx", "head"),
        ),
        out_specs=(P("ctx", "head"), P("ctx", "head"), P("ctx", "head"), P("ctx", "head")),
        check_vma=False,
    )
```

```python
import functools

import jax
import jax.numpy as jnp
from jax import lax
from jax.experimental import pallas as pl
from jax.experimental.pallas import tpu as pltpu
from jax.sharding import PartitionSpec as P

MESH = pl.DeviceIdType.MESH
HIGHEST = lax.Precision.HIGHEST
F32 = jnp.float32
BF16 = jnp.bfloat16
D = 128
HH = 4
HW = HH * D
T2 = 256
W3 = 768
CHANNELS = 4096
SCALE = D ** (-0.5)
BIG = 1e30
PLAN = {
    "p": ("k1a", "q1a"),
    "l": ("k1b", "q1b", "v1a", "g1a", "intra"),
    "e": ("v1b", "g1b", "k2a", "q2a", "k2b", "q2b"),
    "x": ("v2a", "g2a"),
    "o": ("v2b", "g2b", "soft", "ssd"),
    "b": ("query", "early", "late"),
}


def nn(a, b):
    return lax.dot_general(a, b, (((1,), (0,)), ((), ())), preferred_element_type=F32)


def nt(a, b):
    return lax.dot_general(a, b, (((1,), (1,)), ((), ())), preferred_element_type=F32)


def tn(a, b):
    return lax.dot_general(a, b, (((0,), (0,)), ((), ())), preferred_element_type=F32)


def kernel(
    nc, nx,
    q_ref, k_ref, v_ref, g_ref, ld_ref, st_ref, bm_ref,
    om_ref, oq_ref, ok_ref, ov_ref,
    kb, vb, qb, gb, kx, vx, ldb, stb, mk, bmv, part_out, part_in, f_in, l_out, l_in, e_out, e_in,
    o_in, o_out, b_out, b_in, xs, stat, rows, cols, bias, big,
    mix, mixt, pairt, qt, ssd, dss, wq, wk, dq, dk, dv, outs,
    ssem, rsem, lsem,
):
    me = lax.axis_index("ctx")
    x = lax.axis_index("head")
    c = me // 2
    j = me % 2
    part = 512 // nc

    def dev(chip, core, xx):
        return (lax.rem(chip, nc) * 2 + core, xx)

    def order(n):
        half = (n + 1) // 2
        return nc // 2 + jnp.where(n % 2 == 0, half, -half)

    barrier = pltpu.get_barrier_semaphore()

    def greet(n, carry):
        pl.semaphore_signal(barrier, 1, device_id=dev(c + order(n), j, x), device_id_type=MESH)
        return carry

    lax.fori_loop(0, nc - 1, greet, 0)
    greeted = nc - 1
    for other in (dev(c + 1, 1 - j, x), dev(c + nc - 1, 1 - j, x), dev(c, 1 - j, x)):
        pl.semaphore_signal(barrier, 1, device_id=other, device_id_type=MESH)
        greeted += 1
    for step in range(1, nx):
        for core in range(2):
            pl.semaphore_signal(
                barrier, 1, device_id=dev(c, core, lax.rem(x + step, nx)), device_id_type=MESH
            )
            greeted += 1

    sends = []
    count = {"s": 0, "r": 0}

    def slots(kind, n):
        at = count[kind]
        count[kind] += n
        return at

    def remote(src, dst, recv, target):
        copy = pltpu.make_async_remote_copy(
            src_ref=src, dst_ref=dst, send_sem=ssem.at[slots("s", 1)], recv_sem=rsem.at[recv],
            device_id=target, device_id_type=MESH,
        )
        sends.append((copy, src))
        copy.start()

    def arrived(ref, recv):
        pltpu.make_async_copy(ref, ref, rsem.at[recv]).wait()

    mine = pl.ds(pl.multiple_of(j * HW, HW), HW)
    other_half = pl.ds(pl.multiple_of((1 - j) * HW, HW), HW)
    local = []
    for n, (src, dst) in enumerate(
        (
            (ld_ref, ldb.at[j]), (st_ref, stb.at[j]), (bm_ref, bmv),
            (k_ref.at[:, mine], kb.at[2, j]), (v_ref.at[:, mine], vb.at[2, j]),
            (k_ref.at[:, other_half], kx), (v_ref.at[:, other_half], vx),
            (q_ref.at[:, mine], qb.at[0, j]), (g_ref.at[:, mine], gb.at[0, j]),
        )
    ):
        copy = pltpu.make_async_copy(src, dst, lsem.at[n])
        copy.start()
        local.append(copy)
    low = j == 0
    at_row = lax.broadcasted_iota(jnp.int32, (T2, T2), 0)
    at_col = lax.broadcasted_iota(jnp.int32, (T2, T2), 1)
    upper = (at_row <= at_col).astype(F32)
    for copy in local[0:3]:
        copy.wait()
    listed = bmv[...].astype(F32)
    mk[j] = jnp.concatenate(
        [jnp.broadcast_to(listed[:, n : n + 1], (1, D)) for n in range(5)]
        + [jnp.zeros((3, D), F32)],
        axis=0,
    )
    own_prefix = lax.dot_general(
        ldb[j], upper[0:D, 0:D], (((1,), (0,)), ((), ())),
        precision=HIGHEST, preferred_element_type=F32,
    )
    own_carry = jnp.transpose(jnp.exp(own_prefix[:, D - 1 : D] - own_prefix) * stb[j])
    carry_mine = jnp.where(low, own_carry[:, 0:HH], own_carry[:, HH : 2 * HH])
    carry_mate = jnp.where(low, own_carry[:, HH : 2 * HH], own_carry[:, 0:HH])
    for copy in local[3:7]:
        copy.wait()
    for h in range(HH):
        cut = slice(h * D, (h + 1) * D)
        part_out[cut, :] = tn(
            (carry_mate[:, h : h + 1] * kx[:, cut].astype(F32)).astype(BF16), vx[:, cut]
        )
        part_in[j, cut, :] = tn(
            (carry_mine[:, h : h + 1] * kb[2, j, :, cut].astype(F32)).astype(BF16),
            vb[2, j, :, cut],
        )

    pl.semaphore_wait(barrier, greeted)

    mate = dev(c, 1 - j, x)
    small = slots("r", 4)
    remote(ldb.at[j], ldb.at[j], small, mate)
    remote(stb.at[j], stb.at[j], small + 1, mate)
    remote(part_out, part_in.at[j], small + 2, mate)
    remote(mk.at[j], mk.at[j], small + 3, mate)
    swap = slots("r", 4)

    def swap_send(n, src, dst, slot):
        remote(src, dst.at[slot, j], swap + n, mate)

    swap_send(0, kx, kb, 2)
    swap_send(1, vx, vb, 2)
    swap_send(2, q_ref.at[:, other_half], qb, 0)
    swap_send(3, g_ref.at[:, other_half], gb, 0)

    first = slots("r", 16)
    second = slots("r", 16)
    ways = {
        "k": (0, k_ref, kb, 0, 1), "q": (1, q_ref, qb, 2, nc - 1),
        "v": (2, v_ref, vb, 0, 1), "g": (3, g_ref, gb, 2, nc - 1),
    }

    def half(name):
        at = 4 * ways[name[0]][0] + 2 * (name[2] == "b")
        return pl.ds(64 * (name[2] == "b"), 64), first + at, second + at

    def own_on(name):
        _, src, dst, _, step = ways[name[0]]
        lines, near, _ = half(name)
        for core in range(2):
            remote(
                src.at[lines, pl.ds(core * HW, HW)], dst.at[1, j, lines], near + j,
                dev(c + step, core, x),
            )

    def hand_on(name):
        _, _, buf, far, step = ways[name[0]]
        lines, near, later = half(name)
        for core in range(2):
            arrived(buf.at[1, core, lines], near + core)
            remote(
                buf.at[1, core, lines], buf.at[far, core, lines], later + core, dev(c + step, j, x)
            )

    def landed(name):
        _, _, buf, far, _ = ways[name]
        for end in "ab":
            lines, _, later = half(name + "2" + end)
            for core in range(2):
                arrived(buf.at[far, core, lines], later + core)

    acts = {}

    def during(window):
        for item in PLAN[window]:
            if item in acts:
                acts[item]()
            elif item[1] == "1":
                own_on(item)
            else:
                hand_on(item)

    during("p")

    arrived(ldb.at[1 - j], small)
    arrived(stb.at[1 - j], small + 1)
    pair = []
    for ref in (ldb, stb):
        wide = jnp.concatenate([ref[0], ref[1]], axis=1)
        pair.append(jnp.where(low, wide[0:HH], wide[HH : 2 * HH]))
    decay, step_row = pair
    last_wide = jnp.broadcast_to(jnp.sum(decay, axis=1, keepdims=True), (HH, D))
    f_in[pl.ds(c, 1)] = jnp.concatenate([last_wide, last_wide], axis=0)[None]

    def exchange(src_of, dst_of):
        s_at, r_at = slots("s", 1), slots("r", 1)

        def one(n, carry):
            chip = lax.rem(c + order(n), nc)
            pltpu.make_async_remote_copy(
                src_ref=src_of(chip), dst_ref=dst_of(c), send_sem=ssem.at[s_at],
                recv_sem=rsem.at[r_at], device_id=(chip * 2 + j, x), device_id_type=MESH,
            ).start()
            return carry

        lax.fori_loop(0, nc - 1, one, 0, unroll=True)
        return s_at, r_at

    def own(chip):
        return pl.ds(pl.multiple_of(chip * part, part), part)

    def head(ref, slot, h):
        return ref[slot, :, :, h * D : (h + 1) * D].reshape(T2, D)

    def band(ref, h):
        return ref[:, :, :, h * D : (h + 1) * D].reshape(W3, D)

    fade_late = jnp.exp(jnp.sum(decay[:, D : 2 * D], axis=1, keepdims=True))
    arrived(part_in.at[1 - j], small + 2)
    for h in range(HH):
        cut = slice(h * D, (h + 1) * D)
        l_out[cut, :] = (fade_late[h : h + 1, :] * part_in[0, cut, :] + part_in[1, cut, :]).astype(BF16)
    l_sem = exchange(lambda chip: l_out.at[own(chip)], lambda sender: l_in.at[sender])
    l_in[pl.ds(c, 1)] = l_out[own(c), :][None]

    f_sem = exchange(lambda chip: f_in.at[c], lambda sender: f_in.at[sender])

    blank = jnp.full((1, D), BIG, F32)

    def intra():
        prefix = lax.dot_general(
            jnp.concatenate([decay, decay], axis=0), upper, (((1,), (0,)), ((), ())),
            precision=HIGHEST, preferred_element_type=F32,
        )[0:HH]
        last = prefix[:, T2 - 1 : T2]
        carry_row = jnp.exp(last - prefix) * step_row
        packed = jnp.concatenate([prefix, step_row, carry_row, jnp.exp(prefix)], axis=0)
        rows[...] = packed
        cols[...] = jnp.transpose(packed)

        arrived(mk.at[1 - j], small + 3)

        for core in range(2):
            line = []
            for dist in (2, 1, 0):
                for core_k in range(2):
                    off = 2 * dist + core - core_k
                    line.append((1.0 - mk[core, off : off + 1, :]) * BIG if 0 <= off < 5 else blank)
            bias[core : core + 1, :] = jnp.concatenate(line, axis=1) * -1.0

        for copy in local[7:9]:
            copy.wait()
        arrived(kb.at[2, 1 - j], swap)
        arrived(vb.at[2, 1 - j], swap + 1)
        arrived(qb.at[0, 1 - j], swap + 2)
        arrived(gb.at[0, 1 - j], swap + 3)
        for h in range(HH):
            q, k, v = head(qb, 0, h), head(kb, 2, h), head(vb, 2, h)
            p_row, p_col = rows[h : h + 1, :], cols[:, h : h + 1]
            m = jnp.exp(jnp.where(at_row >= at_col, p_col - p_row, -BIG)) * (
                rows[4 + h : 5 + h, :] * SCALE
            )
            mix[h] = m
            ssd[h] = nn((m * nt(q, k)).astype(BF16), v)
            mt = jnp.exp(jnp.where(at_row <= at_col, p_row - p_col, -BIG)) * (
                cols[:, 4 + h : 5 + h] * SCALE
            )
            mixt[h] = mt
            pairt[h] = (mt * nt(k, q)).astype(BF16)
            qt[h] = jnp.transpose(cols[:, 12 + h : 13 + h] * q.astype(F32)).astype(BF16)

    acts["intra"] = intra
    during("l")

    def total(ref):
        return ref.at[pl.ds(0, nc - 1)]

    head_of = c * part // D
    arrived(total(f_in), f_sem[1])
    arrived(total(l_in), l_sem[1])

    def scan(src, dst, reverse):
        def one(n, run):
            chip = nc - 1 - n if reverse else n
            dst[pl.ds(chip, 1)] = run.astype(BF16)[None]
            fade = jnp.exp(f_in[pl.ds(chip, 1), pl.ds(head_of, 1), :][0])
            return fade * run + src[pl.ds(chip, 1)][0].astype(F32)

        lax.fori_loop(0, nc, one, jnp.zeros((part, D), F32), unroll=True)

    scan(l_in, e_out, False)
    e_sem = exchange(lambda chip: e_out.at[chip], lambda sender: e_in.at[own(sender)])
    e_in[own(c), :] = e_out[pl.ds(c, 1)][0]

    during("e")

    rest = e_in.at[pl.ds(0, 512 - part)]
    arrived(rest, e_sem[1])
    squares = jnp.zeros((T2, D), F32)
    inner = jnp.zeros((T2, D), F32)
    for h in range(HH):
        state = e_in[h * D : (h + 1) * D, :]
        y = ssd[h] + (SCALE * cols[:, 12 + h : 13 + h]) * nn(head(qb, 0, h), state)
        ssd[h] = y
        squares = squares + y * y
        inner = inner + y * head(gb, 0, h).astype(F32)
    ones = jnp.ones((8, D), BF16)

    def across(a):
        head_part = a.astype(BF16)
        return nt(ones, head_part) + nt(ones, (a - head_part.astype(F32)).astype(BF16))

    sums = jnp.concatenate([across(squares)[0:4], across(inner)[0:4]], axis=0)
    here = x * 2 + j
    xs[pl.ds(here, 1)] = sums[None]
    x_s, x_r = slots("s", 1), slots("r", 1)
    for step in range(nx):
        for core in range(2):
            if step == 0 and core == 0:
                continue
            pltpu.make_async_remote_copy(
                src_ref=xs.at[here], dst_ref=xs.at[here], send_sem=ssem.at[x_s],
                recv_sem=rsem.at[x_r],
                device_id=dev(c, (j + core) % 2, lax.rem(x + step, nx)), device_id_type=MESH,
            ).start()

    columns = []

    def turned_rows(kinds):
        lane = lax.broadcasted_iota(jnp.int32, (T2, D), 1)
        grid = jnp.zeros((T2, D), F32)
        for n, column in enumerate(kinds):
            grid = jnp.where(lane == n, column, grid)
        return jnp.transpose(grid)[0:8]

    def send_stat(lines, at):
        for dist in (1, 2):
            remote(
                stat.at[0, lines], stat.at[dist, lines], at + dist - 1, dev(c + nc - dist, j, x)
            )

    stat_r = slots("r", 4)

    def soft():
        landed("k")
        for h in range(HH):
            s = nt(head(qb, 0, h), band(kb, h)) * SCALE
            s = (s.reshape(2, D, W3) + bias[0:2, :][:, None, :]).reshape(T2, W3)
            peak = jnp.max(s, axis=-1, keepdims=True)
            e = jnp.exp(s - peak)
            inv = 1.0 / jnp.sum(e, axis=-1, keepdims=True)
            wq[h] = e * inv
            columns.append((peak, inv))
        stat[0, 0:8, :] = turned_rows([p for p, _ in columns] + [i for _, i in columns])
        stat[0, 8:16, :] = jnp.concatenate([mk[0], mk[1]], axis=1)
        send_stat(pl.ds(0, 16), stat_r)

    acts["soft"] = soft
    during("x")

    arrived(xs.at[pl.ds(0, 2 * nx - 1)], x_r)
    both = xs[0]
    for n in range(1, 2 * nx):
        both = both + xs[n]
    inv_root = 1.0 / jnp.sqrt(both[0:4] / CHANNELS + 1e-05)
    cross = both[4:8] * inv_root / CHANNELS
    turned = jnp.transpose(jnp.concatenate([inv_root, inv_root * inv_root * cross], axis=0))
    root_col, slope_col = turned[:, 0:1], turned[:, 4:5]
    for h in range(HH):
        g = head(gb, 0, h).astype(F32)
        y = ssd[h]
        d = (g * root_col - y * slope_col).astype(BF16)
        dss[h] = d
        o_out[h * D : (h + 1) * D, :] = (SCALE * nn(qt[h], d)).astype(BF16)
    o_in[pl.ds(c, 1)] = o_out[own(c), :][None]
    o_sem = exchange(lambda chip: o_out.at[own(chip)], lambda sender: o_in.at[sender])

    out_sends = []
    out_local = []
    out_r = slots("r", 4)

    def emit(n, ref):
        copy = pltpu.make_async_copy(outs.at[n, j], ref.at[:, mine], lsem.at[9 + n])
        copy.start()
        out_local.append(copy)
        far = pltpu.make_async_remote_copy(
            src_ref=outs.at[n, 1 - j], dst_ref=ref.at[:, mine], send_sem=ssem.at[slots("s", 1)],
            recv_sem=rsem.at[out_r + n], device_id=mate, device_id_type=MESH,
        )
        far.start()
        out_sends.append(far)

    def put(n, h, value):
        outs[n, :, :, h * D : (h + 1) * D] = value.astype(BF16).reshape(2, D, D)

    def ssd_grads():
        for h in range(HH):
            q, k, v, d = head(qb, 0, h), head(kb, 2, h), head(vb, 2, h), dss[h]
            state = e_in[h * D : (h + 1) * D, :]
            grad = nn((mix[h] * nt(d, v)).astype(BF16), k)
            grad = grad + (SCALE * cols[:, 12 + h : 13 + h]) * nt(d, state)
            dq[h] = grad
            dk[h] = nn((mixt[h] * nt(v, d)).astype(BF16), q)
            dv[h] = nn(pairt[h], d)

    acts["ssd"] = ssd_grads
    during("o")

    arrived(total(o_in), o_sem[1])
    scan(o_in, b_out, True)
    b_sem = exchange(lambda chip: b_out.at[chip], lambda sender: b_in.at[own(sender)])
    b_in[own(c), :] = b_out[pl.ds(c, 1)][0]

    def query():
        landed("v")
        inners = []
        for h in range(HH):
            g, k, v, w = head(gb, 0, h), band(kb, h), band(vb, h), wq[h]
            a = nn(w.astype(BF16), v)
            row_inner = jnp.sum(g.astype(F32) * a, axis=-1, keepdims=True)
            inners.append(row_inner)
            put(0, h, a + ssd[h] * root_col)
            gs = (SCALE * w * (nt(g, v) - row_inner)).astype(BF16)
            put(1, h, nn(gs, k) + dq[h])
        stat[0, 16:24, :] = turned_rows(inners)
        send_stat(pl.ds(16, 8), stat_r + 2)
        emit(0, om_ref)
        emit(1, oq_ref)

    def early():
        for dist in (1, 2):
            arrived(stat.at[dist, pl.ds(0, 16)], stat_r + dist - 1)
        landed("q")
        for core_k in range(2):
            line = []
            for dist in range(3):
                here_ok = c + dist < nc
                for core in range(2):
                    off = 2 * dist + core - core_k
                    if 0 <= off < 5:
                        listed = stat[dist, 8 + off : 9 + off, core * D : (core + 1) * D]
                        line.append(jnp.where(here_ok, (1.0 - listed) * BIG, BIG))
                    else:
                        line.append(blank)
            big[core_k : core_k + 1, :] = jnp.concatenate(line, axis=1)
        landed("g")
        for h in range(HH):
            q, g, k = band(qb, h), band(gb, h), head(kb, 2, h)
            peak, inv = [
                jnp.concatenate([stat[n, at : at + 1, :] for n in range(3)], axis=1)
                for at in (h, HH + h)
            ]
            shift = peak + big[0:2, :]
            s = nt(k, q) * SCALE
            w = jnp.exp((s.reshape(2, D, W3) - shift[:, None, :]).reshape(T2, W3)) * inv
            dv[h] = dv[h] + nn(w.astype(BF16), g)
            wk[h] = w

    def late():
        for dist in (1, 2):
            arrived(stat.at[dist, pl.ds(16, 8)], stat_r + 1 + dist)
        for h in range(HH):
            row_inner = jnp.concatenate([stat[n, 16 + h : 17 + h, :] for n in range(3)], axis=1)
            gs = (SCALE * wk[h] * (nt(head(vb, 2, h), band(gb, h)) - row_inner)).astype(BF16)
            dk[h] = dk[h] + nn(gs, band(qb, h))

    acts["query"], acts["early"], acts["late"] = query, early, late
    during("b")

    arrived(b_in.at[pl.ds(0, 512 - part)], b_sem[1])
    for h in range(HH):
        state = b_in[h * D : (h + 1) * D, :]
        weight = cols[:, 8 + h : 9 + h]
        put(2, h, dk[h] + weight * nt(head(vb, 2, h), state))
    emit(2, ok_ref)
    for h in range(HH):
        state = b_in[h * D : (h + 1) * D, :]
        weight = cols[:, 8 + h : 9 + h]
        put(3, h, dv[h] + weight * nn(head(kb, 2, h), state))
    emit(3, ov_ref)

    for copy, _ in sends:
        copy.wait_send()
    pltpu.make_async_copy(total(f_in), total(f_in), ssem.at[f_sem[0]]).wait()
    for ref, sem in ((l_in, l_sem), (e_out, e_sem), (o_in, o_sem), (b_out, b_sem)):
        pltpu.make_async_copy(total(ref), total(ref), ssem.at[sem[0]]).wait()
    rest_x = xs.at[pl.ds(0, 2 * nx - 1)]
    pltpu.make_async_copy(rest_x, rest_x, ssem.at[x_s]).wait()
    for copy in out_local:
        copy.wait()
    for copy in out_sends:
        copy.wait()


def store(a, b, c, d, ra, rb, rc, rd, sem):
    copies = [
        pltpu.make_async_copy(src, dst, sem.at[n])
        for n, (src, dst) in enumerate(((a, ra), (b, rb), (c, rc), (d, rd)))
    ]
    for copy in copies:
        copy.start()
    for copy in copies:
        copy.wait()


def solution(mesh):
    nc = mesh.shape["ctx"] // 2
    nx = mesh.shape["head"]
    part = 512 // nc

    def body(query_rows, key_rows, value_rows, log_decay, step_size, band_mask, cotangent):
        tok, width = query_rows.shape
        out = jax.ShapeDtypeStruct((tok, width), BF16)
        hbm = pl.BlockSpec(memory_space=pltpu.HBM)
        band = pltpu.VMEM((3, 2, D, HW), BF16)
        tile2 = pltpu.VMEM((2, 8, D), F32)
        share = pltpu.VMEM((nc, part, D), BF16)
        whole = pltpu.VMEM((HW, D), BF16)
        per_head = pltpu.VMEM((HH, T2, D), F32)
        square = pltpu.VMEM((HH, T2, T2), F32)
        results = pl.pallas_call(
            functools.partial(kernel, nc, nx),
            name="mixer",
            out_shape=(pltpu.VMEM((tok, width), BF16),) * 4,
            in_specs=[hbm] * 7,
            out_specs=(pl.BlockSpec(memory_space=pltpu.VMEM),) * 4,
            scratch_shapes=[
                band, band, band, band, pltpu.VMEM((D, HW), BF16), pltpu.VMEM((D, HW), BF16),
                tile2, tile2, tile2, pltpu.VMEM((1, 5), jnp.int32),
                pltpu.VMEM((HW, D), F32), pltpu.VMEM((2, HW, D), F32), pltpu.VMEM((nc, 8, D), F32),
                whole, share, share, whole,
                share, whole, share, whole,
                pltpu.VMEM((2 * nx, 8, T2), F32), pltpu.VMEM((3, 24, T2), F32),
                pltpu.VMEM((16, T2), F32), pltpu.VMEM((T2, 16), F32),
                pltpu.VMEM((8, W3), F32), pltpu.VMEM((8, W3), F32),
                square, square, pltpu.VMEM((HH, T2, T2), BF16), pltpu.VMEM((HH, D, T2), BF16),
                per_head, pltpu.VMEM((HH, T2, D), BF16),
                pltpu.VMEM((HH, T2, W3), F32), pltpu.VMEM((HH, T2, W3), F32),
                per_head, per_head, per_head,
                pltpu.VMEM((4, 2, D, HW), BF16),
                pltpu.SemaphoreType.DMA((80,)), pltpu.SemaphoreType.DMA((80,)),
                pltpu.SemaphoreType.DMA((16,)),
            ],
            compiler_params=pltpu.CompilerParams(
                collective_id=0, has_side_effects=True, vmem_limit_bytes=56 << 20
            ),
        )(
            *[
                pltpu.with_memory_space_constraint(a, pltpu.HBM)
                for a in (
                    query_rows, key_rows, value_rows, cotangent, log_decay, step_size, band_mask
                )
            ]
        )
        return pl.pallas_call(
            store,
            name="store",
            out_shape=(out,) * 4,
            in_specs=[pl.BlockSpec(memory_space=pltpu.VMEM)] * 4,
            out_specs=(hbm,) * 4,
            scratch_shapes=[pltpu.SemaphoreType.DMA((4,))],
        )(*[pltpu.with_memory_space_constraint(a, pltpu.VMEM) for a in results])

    return jax.shard_map(
        body,
        mesh=mesh,
        in_specs=(
            P("ctx", "head"),
            P("ctx", "head"),
            P("ctx", "head"),
            P("head", "ctx"),
            P("head", "ctx"),
            P("ctx", None),
            P("ctx", "head"),
        ),
        out_specs=(P("ctx", "head"), P("ctx", "head"), P("ctx", "head"), P("ctx", "head")),
        check_vma=False,
    )
```

```python
import functools

import jax
import jax.numpy as jnp
from jax import lax
from jax.experimental import pallas as pl
from jax.experimental.pallas import tpu as pltpu
from jax.sharding import PartitionSpec as P

MESH = pl.DeviceIdType.MESH
HIGHEST = lax.Precision.HIGHEST
F32 = jnp.float32
BF16 = jnp.bfloat16
D = 128
HH = 4
HW = HH * D
T2 = 256
W3 = 768
CHANNELS = 4096
SCALE = D ** (-0.5)
BIG = 1e30
PLAN = {
    "p": ("k1a", "q1a"),
    "l": ("k1b", "q1b", "v1a", "g1a", "intra"),
    "e": ("v1b", "g1b", "k2a", "q2a", "k2b", "q2b"),
    "x": ("v2a", "g2a"),
    "o": ("v2b", "g2b", "soft", "ssd"),
    "b": ("query", "early", "late"),
}


def nn(a, b):
    return lax.dot_general(a, b, (((1,), (0,)), ((), ())), preferred_element_type=F32)


def nt(a, b):
    return lax.dot_general(a, b, (((1,), (1,)), ((), ())), preferred_element_type=F32)


def tn(a, b):
    return lax.dot_general(a, b, (((0,), (0,)), ((), ())), preferred_element_type=F32)


def kernel(
    nc, nx,
    q_ref, k_ref, v_ref, g_ref, ld_ref, st_ref, bm_ref,
    om_ref, oq_ref, ok_ref, ov_ref,
    kb, vb, qb, gb, kx, vx, ldb, stb, mk, bmv, part_out, part_in, f_in, l_out, l_in, e_out, e_in,
    o_in, o_out, b_out, b_in, xs, stat, rows, cols, bias, big,
    mix, mixt, pairt, qt, ssd, dss, wq, wk, dq, dk, dv, outs,
    ssem, rsem, lsem,
):
    me = lax.axis_index("ctx")
    x = lax.axis_index("head")
    c = me // 2
    j = me % 2
    part = 512 // nc

    def dev(chip, core, xx):
        return (lax.rem(chip, nc) * 2 + core, xx)

    def order(n):
        half = (n + 1) // 2
        return nc // 2 + jnp.where(n % 2 == 0, half, -half)

    barrier = pltpu.get_barrier_semaphore()

    def greet(n, carry):
        pl.semaphore_signal(barrier, 1, device_id=dev(c + order(n), j, x), device_id_type=MESH)
        return carry

    lax.fori_loop(0, nc - 1, greet, 0)
    greeted = nc - 1
    for other in (dev(c + 1, 1 - j, x), dev(c + nc - 1, 1 - j, x), dev(c, 1 - j, x)):
        pl.semaphore_signal(barrier, 1, device_id=other, device_id_type=MESH)
        greeted += 1
    for step in range(1, nx):
        for core in range(2):
            pl.semaphore_signal(
                barrier, 1, device_id=dev(c, core, lax.rem(x + step, nx)), device_id_type=MESH
            )
            greeted += 1

    sends = []
    count = {"s": 0, "r": 0}

    def slots(kind, n):
        at = count[kind]
        count[kind] += n
        return at

    def remote(src, dst, recv, target):
        copy = pltpu.make_async_remote_copy(
            src_ref=src, dst_ref=dst, send_sem=ssem.at[slots("s", 1)], recv_sem=rsem.at[recv],
            device_id=target, device_id_type=MESH,
        )
        sends.append((copy, src))
        copy.start()

    def arrived(ref, recv):
        pltpu.make_async_copy(ref, ref, rsem.at[recv]).wait()

    def exchange(src_of, dst_of):
        s_at, r_at = slots("s", 1), slots("r", 1)

        def one(n, carry):
            chip = lax.rem(c + order(n), nc)
            pltpu.make_async_remote_copy(
                src_ref=src_of(chip), dst_ref=dst_of(c), send_sem=ssem.at[s_at],
                recv_sem=rsem.at[r_at], device_id=(chip * 2 + j, x), device_id_type=MESH,
            ).start()
            return carry

        lax.fori_loop(0, nc - 1, one, 0, unroll=True)
        return s_at, r_at

    def own(chip):
        return pl.ds(pl.multiple_of(chip * part, part), part)

    def head(ref, slot, h):
        return ref[slot, :, :, h * D : (h + 1) * D].reshape(T2, D)

    def band(ref, h):
        return ref[:, :, :, h * D : (h + 1) * D].reshape(W3, D)

    mine = pl.ds(pl.multiple_of(j * HW, HW), HW)
    other_half = pl.ds(pl.multiple_of((1 - j) * HW, HW), HW)
    local = []
    for n, (src, dst) in enumerate(
        (
            (ld_ref, ldb.at[j]), (st_ref, stb.at[j]), (bm_ref, bmv),
            (k_ref.at[:, mine], kb.at[2, j]), (v_ref.at[:, mine], vb.at[2, j]),
            (k_ref.at[:, other_half], kx), (v_ref.at[:, other_half], vx),
            (q_ref.at[:, mine], qb.at[0, j]), (g_ref.at[:, mine], gb.at[0, j]),
        )
    ):
        copy = pltpu.make_async_copy(src, dst, lsem.at[n])
        copy.start()
        local.append(copy)
    low = j == 0
    at_row = lax.broadcasted_iota(jnp.int32, (T2, T2), 0)
    at_col = lax.broadcasted_iota(jnp.int32, (T2, T2), 1)
    upper = (at_row <= at_col).astype(F32)
    for copy in local[0:3]:
        copy.wait()
    listed = bmv[...].astype(F32)
    mk[j] = jnp.concatenate(
        [jnp.broadcast_to(listed[:, n : n + 1], (1, D)) for n in range(5)]
        + [jnp.zeros((3, D), F32)],
        axis=0,
    )
    own_prefix = lax.dot_general(
        ldb[j], upper[0:D, 0:D], (((1,), (0,)), ((), ())),
        precision=HIGHEST, preferred_element_type=F32,
    )
    own_last = jnp.broadcast_to(own_prefix[:, D - 1 : D], (8, D))
    f_in[pl.ds(j, 1), pl.ds(c, 1)] = own_last[None, None]
    own_carry = jnp.transpose(jnp.exp(own_prefix[:, D - 1 : D] - own_prefix) * stb[j])
    carry_mine = jnp.where(low, own_carry[:, 0:HH], own_carry[:, HH : 2 * HH])
    carry_mate = jnp.where(low, own_carry[:, HH : 2 * HH], own_carry[:, 0:HH])
    for copy in local[3:7]:
        copy.wait()
    for h in range(HH):
        cut = slice(h * D, (h + 1) * D)
        part_out[cut, :] = tn(
            (carry_mate[:, h : h + 1] * kx[:, cut].astype(F32)).astype(BF16), vx[:, cut]
        )
        part_in[j, cut, :] = tn(
            (carry_mine[:, h : h + 1] * kb[2, j, :, cut].astype(F32)).astype(BF16),
            vb[2, j, :, cut],
        )

    pl.semaphore_wait(barrier, greeted)

    mate = dev(c, 1 - j, x)
    small = slots("r", 4)
    remote(ldb.at[j], ldb.at[j], small, mate)
    remote(stb.at[j], stb.at[j], small + 1, mate)
    remote(part_out, part_in.at[j], small + 2, mate)
    remote(mk.at[j], mk.at[j], small + 3, mate)
    f_sem = exchange(lambda chip: f_in.at[j, c], lambda sender: f_in.at[j, sender])
    swap = slots("r", 4)

    def swap_send(n, src, dst, slot):
        remote(src, dst.at[slot, j], swap + n, mate)

    swap_send(0, kx, kb, 2)
    swap_send(1, vx, vb, 2)
    swap_send(2, q_ref.at[:, other_half], qb, 0)
    swap_send(3, g_ref.at[:, other_half], gb, 0)

    first = slots("r", 16)
    second = slots("r", 16)
    ways = {
        "k": (0, k_ref, kb, 0, 1), "q": (1, q_ref, qb, 2, nc - 1),
        "v": (2, v_ref, vb, 0, 1), "g": (3, g_ref, gb, 2, nc - 1),
    }

    def half(name):
        at = 4 * ways[name[0]][0] + 2 * (name[2] == "b")
        return pl.ds(64 * (name[2] == "b"), 64), first + at, second + at

    def own_on(name):
        _, src, dst, _, step = ways[name[0]]
        lines, near, _ = half(name)
        for core in range(2):
            remote(
                src.at[lines, pl.ds(core * HW, HW)], dst.at[1, j, lines], near + j,
                dev(c + step, core, x),
            )

    def hand_on(name):
        _, _, buf, far, step = ways[name[0]]
        lines, near, later = half(name)
        for core in range(2):
            arrived(buf.at[1, core, lines], near + core)
            remote(
                buf.at[1, core, lines], buf.at[far, core, lines], later + core, dev(c + step, j, x)
            )

    def landed(name):
        _, _, buf, far, _ = ways[name]
        for end in "ab":
            lines, _, later = half(name + "2" + end)
            for core in range(2):
                arrived(buf.at[far, core, lines], later + core)

    acts = {}

    def during(window):
        for item in PLAN[window]:
            if item in acts:
                acts[item]()
            elif item[1] == "1":
                own_on(item)
            else:
                hand_on(item)

    during("p")

    arrived(ldb.at[1 - j], small)
    arrived(stb.at[1 - j], small + 1)
    pair = []
    for ref in (ldb, stb):
        wide = jnp.concatenate([ref[0], ref[1]], axis=1)
        pair.append(jnp.where(low, wide[0:HH], wide[HH : 2 * HH]))
    decay, step_row = pair

    fade_late = jnp.exp(jnp.sum(decay[:, D : 2 * D], axis=1, keepdims=True))
    arrived(part_in.at[1 - j], small + 2)
    for h in range(HH):
        cut = slice(h * D, (h + 1) * D)
        l_out[cut, :] = (fade_late[h : h + 1, :] * part_in[0, cut, :] + part_in[1, cut, :]).astype(BF16)
    l_sem = exchange(lambda chip: l_out.at[own(chip)], lambda sender: l_in.at[sender])
    l_in[pl.ds(c, 1)] = l_out[own(c), :][None]

    blank = jnp.full((1, D), BIG, F32)

    def intra():
        prefix = lax.dot_general(
            jnp.concatenate([decay, decay], axis=0), upper, (((1,), (0,)), ((), ())),
            precision=HIGHEST, preferred_element_type=F32,
        )[0:HH]
        last = prefix[:, T2 - 1 : T2]
        carry_row = jnp.exp(last - prefix) * step_row
        packed = jnp.concatenate([prefix, step_row, carry_row, jnp.exp(prefix)], axis=0)
        rows[...] = packed
        cols[...] = jnp.transpose(packed)

        arrived(mk.at[1 - j], small + 3)

        for core in range(2):
            line = []
            for dist in (2, 1, 0):
                for core_k in range(2):
                    off = 2 * dist + core - core_k
                    line.append((1.0 - mk[core, off : off + 1, :]) * BIG if 0 <= off < 5 else blank)
            bias[core : core + 1, :] = jnp.concatenate(line, axis=1) * -1.0

        for copy in local[7:9]:
            copy.wait()
        arrived(kb.at[2, 1 - j], swap)
        arrived(vb.at[2, 1 - j], swap + 1)
        arrived(qb.at[0, 1 - j], swap + 2)
        arrived(gb.at[0, 1 - j], swap + 3)
        for h in range(HH):
            q, k, v = head(qb, 0, h), head(kb, 2, h), head(vb, 2, h)
            p_row, p_col = rows[h : h + 1, :], cols[:, h : h + 1]
            m = jnp.exp(jnp.where(at_row >= at_col, p_col - p_row, -BIG)) * (
                rows[4 + h : 5 + h, :] * SCALE
            )
            mix[h] = m
            ssd[h] = nn((m * nt(q, k)).astype(BF16), v)
            mt = jnp.exp(jnp.where(at_row <= at_col, p_row - p_col, -BIG)) * (
                cols[:, 4 + h : 5 + h] * SCALE
            )
            mixt[h] = mt
            pairt[h] = (mt * nt(k, q)).astype(BF16)
            qt[h] = jnp.transpose(cols[:, 12 + h : 13 + h] * q.astype(F32)).astype(BF16)

    acts["intra"] = intra
    during("l")

    def total(ref):
        return ref.at[pl.ds(0, nc - 1)]

    row_of = j * HH + c * part // D
    f_mate = slots("r", 1)
    f_own = f_in.at[j, pl.ds(0, nc - 1)]
    arrived(f_own, f_sem[1])
    remote(f_in.at[j], f_in.at[j], f_mate, mate)
    arrived(f_in.at[1 - j], f_mate)
    arrived(total(l_in), l_sem[1])

    def scan(src, dst, reverse):
        def one(n, run):
            chip = nc - 1 - n if reverse else n
            dst[pl.ds(chip, 1)] = run.astype(BF16)[None]
            fade = jnp.exp(
                f_in[0, pl.ds(chip, 1), pl.ds(row_of, 1), :][0]
                + f_in[1, pl.ds(chip, 1), pl.ds(row_of, 1), :][0]
            )
            return fade * run + src[pl.ds(chip, 1)][0].astype(F32)

        lax.fori_loop(0, nc, one, jnp.zeros((part, D), F32), unroll=True)

    scan(l_in, e_out, False)
    e_sem = exchange(lambda chip: e_out.at[chip], lambda sender: e_in.at[own(sender)])
    e_in[own(c), :] = e_out[pl.ds(c, 1)][0]

    during("e")

    rest = e_in.at[pl.ds(0, 512 - part)]
    arrived(rest, e_sem[1])
    squares = jnp.zeros((T2, D), F32)
    inner = jnp.zeros((T2, D), F32)
    for h in range(HH):
        state = e_in[h * D : (h + 1) * D, :]
        y = ssd[h] + (SCALE * cols[:, 12 + h : 13 + h]) * nn(head(qb, 0, h), state)
        ssd[h] = y
        squares = squares + y * y
        inner = inner + y * head(gb, 0, h).astype(F32)
    ones = jnp.ones((8, D), BF16)

    def across(a):
        head_part = a.astype(BF16)
        return nt(ones, head_part) + nt(ones, (a - head_part.astype(F32)).astype(BF16))

    sums = jnp.concatenate([across(squares)[0:4], across(inner)[0:4]], axis=0)
    here = x * 2 + j
    xs[pl.ds(here, 1)] = sums[None]
    x_s, x_r = slots("s", 1), slots("r", 1)
    for step in range(nx):
        for core in range(2):
            if step == 0 and core == 0:
                continue
            pltpu.make_async_remote_copy(
                src_ref=xs.at[here], dst_ref=xs.at[here], send_sem=ssem.at[x_s],
                recv_sem=rsem.at[x_r],
                device_id=dev(c, (j + core) % 2, lax.rem(x + step, nx)), device_id_type=MESH,
            ).start()

    columns = []

    def turned_rows(kinds):
        lane = lax.broadcasted_iota(jnp.int32, (T2, D), 1)
        grid = jnp.zeros((T2, D), F32)
        for n, column in enumerate(kinds):
            grid = jnp.where(lane == n, column, grid)
        return jnp.transpose(grid)[0:8]

    def send_stat(lines, at):
        for dist in (1, 2):
            remote(
                stat.at[0, lines], stat.at[dist, lines], at + dist - 1, dev(c + nc - dist, j, x)
            )

    stat_r = slots("r", 4)

    def soft():
        landed("k")
        for h in range(HH):
            s = nt(head(qb, 0, h), band(kb, h)) * SCALE
            s = (s.reshape(2, D, W3) + bias[0:2, :][:, None, :]).reshape(T2, W3)
            peak = jnp.max(s, axis=-1, keepdims=True)
            e = jnp.exp(s - peak)
            inv = 1.0 / jnp.sum(e, axis=-1, keepdims=True)
            wq[h] = e * inv
            columns.append((peak, inv))
        stat[0, 0:8, :] = turned_rows([p for p, _ in columns] + [i for _, i in columns])
        stat[0, 8:16, :] = jnp.concatenate([mk[0], mk[1]], axis=1)
        send_stat(pl.ds(0, 16), stat_r)

    acts["soft"] = soft
    during("x")

    arrived(xs.at[pl.ds(0, 2 * nx - 1)], x_r)
    both = xs[0]
    for n in range(1, 2 * nx):
        both = both + xs[n]
    inv_root = 1.0 / jnp.sqrt(both[0:4] / CHANNELS + 1e-05)
    cross = both[4:8] * inv_root / CHANNELS
    turned = jnp.transpose(jnp.concatenate([inv_root, inv_root * inv_root * cross], axis=0))
    root_col, slope_col = turned[:, 0:1], turned[:, 4:5]
    for h in range(HH):
        g = head(gb, 0, h).astype(F32)
        y = ssd[h]
        d = (g * root_col - y * slope_col).astype(BF16)
        dss[h] = d
        o_out[h * D : (h + 1) * D, :] = (SCALE * nn(qt[h], d)).astype(BF16)
    o_in[pl.ds(c, 1)] = o_out[own(c), :][None]
    o_sem = exchange(lambda chip: o_out.at[own(chip)], lambda sender: o_in.at[sender])

    out_sends = []
    out_local = []
    out_r = slots("r", 4)

    def emit(n, ref):
        copy = pltpu.make_async_copy(outs.at[n, j], ref.at[:, mine], lsem.at[9 + n])
        copy.start()
        out_local.append(copy)
        emit_far(n, ref)

    def emit_far(n, ref):
        far = pltpu.make_async_remote_copy(
            src_ref=outs.at[n, 1 - j], dst_ref=ref.at[:, mine], send_sem=ssem.at[slots("s", 1)],
            recv_sem=rsem.at[out_r + n], device_id=mate, device_id_type=MESH,
        )
        far.start()
        out_sends.append(far)

    def put(n, h, value):
        outs[n, :, :, h * D : (h + 1) * D] = value.astype(BF16).reshape(2, D, D)

    def ssd_grads():
        for h in range(HH):
            q, k, v, d = head(qb, 0, h), head(kb, 2, h), head(vb, 2, h), dss[h]
            state = e_in[h * D : (h + 1) * D, :]
            grad = nn((mix[h] * nt(d, v)).astype(BF16), k)
            grad = grad + (SCALE * cols[:, 12 + h : 13 + h]) * nt(d, state)
            dq[h] = grad
            dk[h] = nn((mixt[h] * nt(v, d)).astype(BF16), q)
            dv[h] = nn(pairt[h], d)

    acts["ssd"] = ssd_grads
    during("o")

    arrived(total(o_in), o_sem[1])
    scan(o_in, b_out, True)
    b_sem = exchange(lambda chip: b_out.at[chip], lambda sender: b_in.at[own(sender)])
    b_in[own(c), :] = b_out[pl.ds(c, 1)][0]

    def query():
        landed("v")
        inners = []
        for h in range(HH):
            g, k, v, w = head(gb, 0, h), band(kb, h), band(vb, h), wq[h]
            a = nn(w.astype(BF16), v)
            row_inner = jnp.sum(g.astype(F32) * a, axis=-1, keepdims=True)
            inners.append(row_inner)
            put(0, h, a + ssd[h] * root_col)
            gs = (SCALE * w * (nt(g, v) - row_inner)).astype(BF16)
            put(1, h, nn(gs, k) + dq[h])
        stat[0, 16:24, :] = turned_rows(inners)
        send_stat(pl.ds(16, 8), stat_r + 2)
        emit(0, om_ref)
        emit(1, oq_ref)

    def early():
        for dist in (1, 2):
            arrived(stat.at[dist, pl.ds(0, 16)], stat_r + dist - 1)
        landed("q")
        for core_k in range(2):
            line = []
            for dist in range(3):
                here_ok = c + dist < nc
                for core in range(2):
                    off = 2 * dist + core - core_k
                    if 0 <= off < 5:
                        listed = stat[dist, 8 + off : 9 + off, core * D : (core + 1) * D]
                        line.append(jnp.where(here_ok, (1.0 - listed) * BIG, BIG))
                    else:
                        line.append(blank)
            big[core_k : core_k + 1, :] = jnp.concatenate(line, axis=1)
        landed("g")
        for h in range(HH):
            q, g, k = band(qb, h), band(gb, h), head(kb, 2, h)
            peak, inv = [
                jnp.concatenate([stat[n, at : at + 1, :] for n in range(3)], axis=1)
                for at in (h, HH + h)
            ]
            shift = peak + big[0:2, :]
            s = nt(k, q) * SCALE
            w = jnp.exp((s.reshape(2, D, W3) - shift[:, None, :]).reshape(T2, W3)) * inv
            dv[h] = dv[h] + nn(w.astype(BF16), g)
            wk[h] = w

    def late():
        for dist in (1, 2):
            arrived(stat.at[dist, pl.ds(16, 8)], stat_r + 1 + dist)
        for h in range(HH):
            row_inner = jnp.concatenate([stat[n, 16 + h : 17 + h, :] for n in range(3)], axis=1)
            gs = (SCALE * wk[h] * (nt(head(vb, 2, h), band(gb, h)) - row_inner)).astype(BF16)
            dk[h] = dk[h] + nn(gs, band(qb, h))

    acts["query"], acts["early"], acts["late"] = query, early, late
    during("b")

    arrived(b_in.at[pl.ds(0, 512 - part)], b_sem[1])
    def finish(block, store):
        at = pl.ds(pl.multiple_of(block * D, D), D)
        for h in range(HH):
            cut = slice(h * D, (h + 1) * D)
            state = b_in[cut, :]
            weight = cols[at, 8 + h : 9 + h]
            store(2, h, dk[h, at, :] + weight * nt(vb[2, block, :, cut], state))
            store(3, h, dv[h, at, :] + weight * nn(kb[2, block, :, cut], state))

    def for_mate(n, h, value):
        outs[n, 1 - j, :, h * D : (h + 1) * D] = value.astype(BF16)

    def for_here(n, h, value):
        ref = (ok_ref, ov_ref)[n - 2]
        ref[:, pl.ds(pl.multiple_of(j * HW + h * D, D), D)] = value.astype(BF16)

    finish(1 - j, for_mate)
    emit_far(2, ok_ref)
    emit_far(3, ov_ref)
    finish(j, for_here)

    for copy, _ in sends:
        copy.wait_send()
    pltpu.make_async_copy(f_own, f_own, ssem.at[f_sem[0]]).wait()
    for ref, sem in ((l_in, l_sem), (e_out, e_sem), (o_in, o_sem), (b_out, b_sem)):
        pltpu.make_async_copy(total(ref), total(ref), ssem.at[sem[0]]).wait()
    rest_x = xs.at[pl.ds(0, 2 * nx - 1)]
    pltpu.make_async_copy(rest_x, rest_x, ssem.at[x_s]).wait()
    for copy in out_local:
        copy.wait()
    for copy in out_sends:
        copy.wait()


def store(a, b, c, d, ra, rb, rc, rd, sem):
    copies = [
        pltpu.make_async_copy(src, dst, sem.at[n])
        for n, (src, dst) in enumerate(((a, ra), (b, rb), (c, rc), (d, rd)))
    ]
    for copy in copies:
        copy.start()
    for copy in copies:
        copy.wait()


def solution(mesh):
    nc = mesh.shape["ctx"] // 2
    nx = mesh.shape["head"]
    part = 512 // nc

    def body(query_rows, key_rows, value_rows, log_decay, step_size, band_mask, cotangent):
        tok, width = query_rows.shape
        out = jax.ShapeDtypeStruct((tok, width), BF16)
        hbm = pl.BlockSpec(memory_space=pltpu.HBM)
        band = pltpu.VMEM((3, 2, D, HW), BF16)
        tile2 = pltpu.VMEM((2, 8, D), F32)
        share = pltpu.VMEM((nc, part, D), BF16)
        whole = pltpu.VMEM((HW, D), BF16)
        per_head = pltpu.VMEM((HH, T2, D), F32)
        square = pltpu.VMEM((HH, T2, T2), F32)
        results = pl.pallas_call(
            functools.partial(kernel, nc, nx),
            name="mixer",
            out_shape=(pltpu.VMEM((tok, width), BF16),) * 4,
            in_specs=[hbm] * 7,
            out_specs=(pl.BlockSpec(memory_space=pltpu.VMEM),) * 4,
            scratch_shapes=[
                band, band, band, band, pltpu.VMEM((D, HW), BF16), pltpu.VMEM((D, HW), BF16),
                tile2, tile2, tile2, pltpu.VMEM((1, 5), jnp.int32),
                pltpu.VMEM((HW, D), F32), pltpu.VMEM((2, HW, D), F32), pltpu.VMEM((2, nc, 8, D), F32),
                whole, share, share, whole,
                share, whole, share, whole,
                pltpu.VMEM((2 * nx, 8, T2), F32), pltpu.VMEM((3, 24, T2), F32),
                pltpu.VMEM((16, T2), F32), pltpu.VMEM((T2, 16), F32),
                pltpu.VMEM((8, W3), F32), pltpu.VMEM((8, W3), F32),
                square, square, pltpu.VMEM((HH, T2, T2), BF16), pltpu.VMEM((HH, D, T2), BF16),
                per_head, pltpu.VMEM((HH, T2, D), BF16),
                pltpu.VMEM((HH, T2, W3), F32), pltpu.VMEM((HH, T2, W3), F32),
                per_head, per_head, per_head,
                pltpu.VMEM((4, 2, D, HW), BF16),
                pltpu.SemaphoreType.DMA((80,)), pltpu.SemaphoreType.DMA((80,)),
                pltpu.SemaphoreType.DMA((16,)),
            ],
            compiler_params=pltpu.CompilerParams(
                collective_id=0, has_side_effects=True, vmem_limit_bytes=56 << 20
            ),
        )(
            *[
                pltpu.with_memory_space_constraint(a, pltpu.HBM)
                for a in (
                    query_rows, key_rows, value_rows, cotangent, log_decay, step_size, band_mask
                )
            ]
        )
        return pl.pallas_call(
            store,
            name="store",
            out_shape=(out,) * 4,
            in_specs=[pl.BlockSpec(memory_space=pltpu.VMEM)] * 4,
            out_specs=(hbm,) * 4,
            scratch_shapes=[pltpu.SemaphoreType.DMA((4,))],
        )(*[pltpu.with_memory_space_constraint(a, pltpu.VMEM) for a in results])

    return jax.shard_map(
        body,
        mesh=mesh,
        in_specs=(
            P("ctx", "head"),
            P("ctx", "head"),
            P("ctx", "head"),
            P("head", "ctx"),
            P("head", "ctx"),
            P("ctx", None),
            P("ctx", "head"),
        ),
        out_specs=(P("ctx", "head"), P("ctx", "head"), P("ctx", "head"), P("ctx", "head")),
        check_vma=False,
    )
```

```python
import functools

import jax
import jax.numpy as jnp
from jax import lax
from jax.experimental import pallas as pl
from jax.experimental.pallas import tpu as pltpu
from jax.sharding import PartitionSpec as P

MESH = pl.DeviceIdType.MESH
HIGHEST = lax.Precision.HIGHEST
F32 = jnp.float32
BF16 = jnp.bfloat16
D = 128
HH = 4
HW = HH * D
T2 = 256
W3 = 768
CHANNELS = 4096
SCALE = D ** (-0.5)
BIG = 1e30
PLAN = {
    "p": ("k1a", "q1a"),
    "l": ("k1b", "q1b", "v1a", "g1a", "intra"),
    "e": ("v1b", "g1b", "k2a", "k2b", "q2a"),
    "x": ("v2a", "q2b"),
    "o": ("v2b", "g2a", "g2b", "soft", "ssd"),
    "b": ("query", "early", "late"),
}


def nn(a, b):
    return lax.dot_general(a, b, (((1,), (0,)), ((), ())), preferred_element_type=F32)


def nt(a, b):
    return lax.dot_general(a, b, (((1,), (1,)), ((), ())), preferred_element_type=F32)


def tn(a, b):
    return lax.dot_general(a, b, (((0,), (0,)), ((), ())), preferred_element_type=F32)


def kernel(
    nc, nx,
    q_ref, k_ref, v_ref, g_ref, ld_ref, st_ref, bm_ref,
    om_ref, oq_ref, ok_ref, ov_ref,
    kb, vb, qb, gb, kx, vx, ldb, stb, mk, bmv, part_out, part_in, f_in, l_out, l_in, e_out, e_in,
    o_in, o_out, b_out, b_in, xs, stat, rows, cols, bias, big,
    mix, mixt, pairt, qt, ssd, dss, wq, wk, dq, dk, dv, outs,
    ssem, rsem, lsem,
):
    me = lax.axis_index("ctx")
    x = lax.axis_index("head")
    c = me // 2
    j = me % 2
    part = 512 // nc

    def dev(chip, core, xx):
        return (lax.rem(chip, nc) * 2 + core, xx)

    def order(n):
        half = (n + 1) // 2
        return nc // 2 + jnp.where(n % 2 == 0, half, -half)

    barrier = pltpu.get_barrier_semaphore()

    def greet(n, carry):
        pl.semaphore_signal(barrier, 1, device_id=dev(c + order(n), j, x), device_id_type=MESH)
        return carry

    lax.fori_loop(0, nc - 1, greet, 0)
    greeted = nc - 1
    pl.semaphore_signal(barrier, 1, device_id=dev(c, 1 - j, x), device_id_type=MESH)
    greeted += 1
    for step in range(1, nx):
        for core in range(2):
            pl.semaphore_signal(
                barrier, 1, device_id=dev(c, core, lax.rem(x + step, nx)), device_id_type=MESH
            )
            greeted += 1

    sends = []
    count = {"s": 0, "r": 0}

    def slots(kind, n):
        at = count[kind]
        count[kind] += n
        return at

    def remote(src, dst, recv, target):
        copy = pltpu.make_async_remote_copy(
            src_ref=src, dst_ref=dst, send_sem=ssem.at[slots("s", 1)], recv_sem=rsem.at[recv],
            device_id=target, device_id_type=MESH,
        )
        sends.append((copy, src))
        copy.start()

    def arrived(ref, recv):
        pltpu.make_async_copy(ref, ref, rsem.at[recv]).wait()

    def exchange(src_of, dst_of):
        s_at, r_at = slots("s", 1), slots("r", 1)

        def one(n, carry):
            chip = lax.rem(c + order(n), nc)
            pltpu.make_async_remote_copy(
                src_ref=src_of(chip), dst_ref=dst_of(c), send_sem=ssem.at[s_at],
                recv_sem=rsem.at[r_at], device_id=(chip * 2 + j, x), device_id_type=MESH,
            ).start()
            return carry

        lax.fori_loop(0, nc - 1, one, 0, unroll=True)
        return s_at, r_at

    def own(chip):
        return pl.ds(pl.multiple_of(chip * part, part), part)

    def head(ref, slot, h):
        return ref[slot, :, :, h * D : (h + 1) * D].reshape(T2, D)

    def band(ref, h):
        return ref[:, :, :, h * D : (h + 1) * D].reshape(W3, D)

    mine = pl.ds(pl.multiple_of(j * HW, HW), HW)
    other_half = pl.ds(pl.multiple_of((1 - j) * HW, HW), HW)
    local = []
    for n, (src, dst) in enumerate(
        (
            (ld_ref, ldb.at[j]), (st_ref, stb.at[j]), (bm_ref, bmv),
            (k_ref.at[:, mine], kb.at[2, j]), (v_ref.at[:, mine], vb.at[2, j]),
            (k_ref.at[:, other_half], kx), (v_ref.at[:, other_half], vx),
            (q_ref.at[:, mine], qb.at[0, j]), (g_ref.at[:, mine], gb.at[0, j]),
        )
    ):
        copy = pltpu.make_async_copy(src, dst, lsem.at[n])
        copy.start()
        local.append(copy)
    low = j == 0
    at_row = lax.broadcasted_iota(jnp.int32, (T2, T2), 0)
    at_col = lax.broadcasted_iota(jnp.int32, (T2, T2), 1)
    upper = (at_row <= at_col).astype(F32)
    for copy in local[0:3]:
        copy.wait()
    listed = bmv[...].astype(F32)
    mk[j] = jnp.concatenate(
        [jnp.broadcast_to(listed[:, n : n + 1], (1, D)) for n in range(5)]
        + [jnp.zeros((3, D), F32)],
        axis=0,
    )
    own_prefix = lax.dot_general(
        ldb[j], upper[0:D, 0:D], (((1,), (0,)), ((), ())),
        precision=HIGHEST, preferred_element_type=F32,
    )
    own_last = jnp.broadcast_to(own_prefix[:, D - 1 : D], (8, D))
    f_in[pl.ds(j, 1), pl.ds(c, 1)] = own_last[None, None]
    own_carry = jnp.transpose(jnp.exp(own_prefix[:, D - 1 : D] - own_prefix) * stb[j])
    carry_mine = jnp.where(low, own_carry[:, 0:HH], own_carry[:, HH : 2 * HH])
    carry_mate = jnp.where(low, own_carry[:, HH : 2 * HH], own_carry[:, 0:HH])
    for copy in local[3:7]:
        copy.wait()
    for h in range(HH):
        cut = slice(h * D, (h + 1) * D)
        part_out[cut, :] = tn(
            (carry_mate[:, h : h + 1] * kx[:, cut].astype(F32)).astype(BF16), vx[:, cut]
        )
        part_in[j, cut, :] = tn(
            (carry_mine[:, h : h + 1] * kb[2, j, :, cut].astype(F32)).astype(BF16),
            vb[2, j, :, cut],
        )

    pl.semaphore_wait(barrier, greeted)

    mate = dev(c, 1 - j, x)
    small = slots("r", 4)
    remote(ldb.at[j], ldb.at[j], small, mate)
    remote(stb.at[j], stb.at[j], small + 1, mate)
    remote(part_out, part_in.at[j], small + 2, mate)
    remote(mk.at[j], mk.at[j], small + 3, mate)
    f_sem = exchange(lambda chip: f_in.at[j, c], lambda sender: f_in.at[j, sender])
    swap = slots("r", 4)

    def swap_send(n, src, dst, slot):
        remote(src, dst.at[slot, j], swap + n, mate)

    swap_send(0, kx, kb, 2)
    swap_send(1, vx, vb, 2)
    swap_send(2, q_ref.at[:, other_half], qb, 0)
    swap_send(3, g_ref.at[:, other_half], gb, 0)

    first = slots("r", 8)
    second = slots("r", 8)
    ways = {
        "k": (0, k_ref, kb, 2, 0, 1), "v": (1, v_ref, vb, 2, 0, 1),
        "q": (2, q_ref, qb, 0, 2, nc - 1), "g": (3, g_ref, gb, 0, 2, nc - 1),
    }
    swapped = set()

    def have(name):
        n, _, buf, slot, _, _ = ways[name]
        if name not in swapped:
            swapped.add(name)
            arrived(buf.at[slot, 1 - j], swap + n)

    def place(name):
        mates = name[2] == "b"
        at = 2 * ways[name[0]][0] + mates
        return (1 - j if mates else j), first + at, second + at

    def own_on(name):
        _, src, buf, slot, _, step = ways[name[0]]
        block, near, _ = place(name)
        if name[2] == "b":
            have(name[0])
            src = buf.at[slot, block]
        else:
            src = src.at[:, mine]
        remote(src, buf.at[1, block], near, dev(c + step, j, x))

    def hand_on(name):
        _, _, buf, _, far, step = ways[name[0]]
        block, near, later = place(name)
        arrived(buf.at[1, block], near)
        remote(buf.at[1, block], buf.at[far, block], later, dev(c + step, j, x))

    def landed(name):
        _, _, buf, _, far, _ = ways[name]
        for end in "ab":
            block, _, later = place(name + "2" + end)
            arrived(buf.at[far, block], later)

    acts = {}

    def during(window):
        for item in PLAN[window]:
            if item in acts:
                acts[item]()
            elif item[1] == "1":
                own_on(item)
            else:
                hand_on(item)

    during("p")

    arrived(ldb.at[1 - j], small)
    arrived(stb.at[1 - j], small + 1)
    pair = []
    for ref in (ldb, stb):
        wide = jnp.concatenate([ref[0], ref[1]], axis=1)
        pair.append(jnp.where(low, wide[0:HH], wide[HH : 2 * HH]))
    decay, step_row = pair

    fade_late = jnp.exp(jnp.sum(decay[:, D : 2 * D], axis=1, keepdims=True))
    arrived(part_in.at[1 - j], small + 2)
    for h in range(HH):
        cut = slice(h * D, (h + 1) * D)
        l_out[cut, :] = (fade_late[h : h + 1, :] * part_in[0, cut, :] + part_in[1, cut, :]).astype(BF16)
    l_sem = exchange(lambda chip: l_out.at[own(chip)], lambda sender: l_in.at[sender])
    l_in[pl.ds(c, 1)] = l_out[own(c), :][None]

    blank = jnp.full((1, D), BIG, F32)

    def intra():
        prefix = lax.dot_general(
            jnp.concatenate([decay, decay], axis=0), upper, (((1,), (0,)), ((), ())),
            precision=HIGHEST, preferred_element_type=F32,
        )[0:HH]
        last = prefix[:, T2 - 1 : T2]
        carry_row = jnp.exp(last - prefix) * step_row
        packed = jnp.concatenate([prefix, step_row, carry_row, jnp.exp(prefix)], axis=0)
        rows[...] = packed
        cols[...] = jnp.transpose(packed)

        arrived(mk.at[1 - j], small + 3)

        for core in range(2):
            line = []
            for dist in (2, 1, 0):
                for core_k in range(2):
                    off = 2 * dist + core - core_k
                    line.append((1.0 - mk[core, off : off + 1, :]) * BIG if 0 <= off < 5 else blank)
            bias[core : core + 1, :] = jnp.concatenate(line, axis=1) * -1.0

        for copy in local[7:9]:
            copy.wait()
        for name in ways:
            have(name)
        for h in range(HH):
            q, k, v = head(qb, 0, h), head(kb, 2, h), head(vb, 2, h)
            p_row, p_col = rows[h : h + 1, :], cols[:, h : h + 1]
            m = jnp.exp(jnp.where(at_row >= at_col, p_col - p_row, -BIG)) * (
                rows[4 + h : 5 + h, :] * SCALE
            )
            mix[h] = m
            ssd[h] = nn((m * nt(q, k)).astype(BF16), v)
            mt = jnp.exp(jnp.where(at_row <= at_col, p_row - p_col, -BIG)) * (
                cols[:, 4 + h : 5 + h] * SCALE
            )
            mixt[h] = mt
            pairt[h] = (mt * nt(k, q)).astype(BF16)
            qt[h] = jnp.transpose(cols[:, 12 + h : 13 + h] * q.astype(F32)).astype(BF16)

    acts["intra"] = intra
    during("l")

    def total(ref):
        return ref.at[pl.ds(0, nc - 1)]

    row_of = j * HH + c * part // D
    f_mate = slots("r", 1)
    f_own = f_in.at[j, pl.ds(0, nc - 1)]
    arrived(f_own, f_sem[1])
    remote(f_in.at[j], f_in.at[j], f_mate, mate)
    arrived(f_in.at[1 - j], f_mate)
    arrived(total(l_in), l_sem[1])

    def scan(src, dst, reverse):
        def one(n, run):
            chip = nc - 1 - n if reverse else n
            dst[pl.ds(chip, 1)] = run.astype(BF16)[None]
            fade = jnp.exp(
                f_in[0, pl.ds(chip, 1), pl.ds(row_of, 1), :][0]
                + f_in[1, pl.ds(chip, 1), pl.ds(row_of, 1), :][0]
            )
            return fade * run + src[pl.ds(chip, 1)][0].astype(F32)

        lax.fori_loop(0, nc, one, jnp.zeros((part, D), F32), unroll=True)

    scan(l_in, e_out, False)
    e_sem = exchange(lambda chip: e_out.at[chip], lambda sender: e_in.at[own(sender)])
    e_in[own(c), :] = e_out[pl.ds(c, 1)][0]

    during("e")

    rest = e_in.at[pl.ds(0, 512 - part)]
    arrived(rest, e_sem[1])
    squares = jnp.zeros((T2, D), F32)
    inner = jnp.zeros((T2, D), F32)
    for h in range(HH):
        state = e_in[h * D : (h + 1) * D, :]
        y = ssd[h] + (SCALE * cols[:, 12 + h : 13 + h]) * nn(head(qb, 0, h), state)
        ssd[h] = y
        squares = squares + y * y
        inner = inner + y * head(gb, 0, h).astype(F32)
    ones = jnp.ones((8, D), BF16)

    def across(a):
        head_part = a.astype(BF16)
        return nt(ones, head_part) + nt(ones, (a - head_part.astype(F32)).astype(BF16))

    sums = jnp.concatenate([across(squares)[0:4], across(inner)[0:4]], axis=0)
    here = x * 2 + j
    xs[pl.ds(here, 1)] = sums[None]
    x_s, x_r = slots("s", 1), slots("r", 1)
    for step in range(nx):
        for core in range(2):
            if step == 0 and core == 0:
                continue
            pltpu.make_async_remote_copy(
                src_ref=xs.at[here], dst_ref=xs.at[here], send_sem=ssem.at[x_s],
                recv_sem=rsem.at[x_r],
                device_id=dev(c, (j + core) % 2, lax.rem(x + step, nx)), device_id_type=MESH,
            ).start()

    columns = []

    def turned_rows(kinds):
        lane = lax.broadcasted_iota(jnp.int32, (T2, D), 1)
        grid = jnp.zeros((T2, D), F32)
        for n, column in enumerate(kinds):
            grid = jnp.where(lane == n, column, grid)
        return jnp.transpose(grid)[0:8]

    def send_stat(lines, at):
        for dist in (1, 2):
            remote(
                stat.at[0, lines], stat.at[dist, lines], at + dist - 1, dev(c + nc - dist, j, x)
            )

    stat_r = slots("r", 4)

    def soft():
        landed("k")
        for h in range(HH):
            s = nt(head(qb, 0, h), band(kb, h)) * SCALE
            s = (s.reshape(2, D, W3) + bias[0:2, :][:, None, :]).reshape(T2, W3)
            peak = jnp.max(s, axis=-1, keepdims=True)
            e = jnp.exp(s - peak)
            inv = 1.0 / jnp.sum(e, axis=-1, keepdims=True)
            wq[h] = e * inv
            columns.append((peak, inv))
        stat[0, 0:8, :] = turned_rows([p for p, _ in columns] + [i for _, i in columns])
        stat[0, 8:16, :] = jnp.concatenate([mk[0], mk[1]], axis=1)
        send_stat(pl.ds(0, 16), stat_r)

    acts["soft"] = soft
    during("x")

    arrived(xs.at[pl.ds(0, 2 * nx - 1)], x_r)
    both = xs[0]
    for n in range(1, 2 * nx):
        both = both + xs[n]
    inv_root = 1.0 / jnp.sqrt(both[0:4] / CHANNELS + 1e-05)
    cross = both[4:8] * inv_root / CHANNELS
    turned = jnp.transpose(jnp.concatenate([inv_root, inv_root * inv_root * cross], axis=0))
    root_col, slope_col = turned[:, 0:1], turned[:, 4:5]
    for h in range(HH):
        g = head(gb, 0, h).astype(F32)
        y = ssd[h]
        d = (g * root_col - y * slope_col).astype(BF16)
        dss[h] = d
        o_out[h * D : (h + 1) * D, :] = (SCALE * nn(qt[h], d)).astype(BF16)
    o_in[pl.ds(c, 1)] = o_out[own(c), :][None]
    o_sem = exchange(lambda chip: o_out.at[own(chip)], lambda sender: o_in.at[sender])

    out_sends = []
    out_local = []
    out_r = slots("r", 4)

    def emit(n, ref):
        copy = pltpu.make_async_copy(outs.at[n, j], ref.at[:, mine], lsem.at[9 + n])
        copy.start()
        out_local.append(copy)
        emit_far(n, ref)

    def emit_far(n, ref):
        far = pltpu.make_async_remote_copy(
            src_ref=outs.at[n, 1 - j], dst_ref=ref.at[:, mine], send_sem=ssem.at[slots("s", 1)],
            recv_sem=rsem.at[out_r + n], device_id=mate, device_id_type=MESH,
        )
        far.start()
        out_sends.append(far)

    def put(n, h, value):
        outs[n, :, :, h * D : (h + 1) * D] = value.astype(BF16).reshape(2, D, D)

    def ssd_grads():
        for h in range(HH):
            q, k, v, d = head(qb, 0, h), head(kb, 2, h), head(vb, 2, h), dss[h]
            state = e_in[h * D : (h + 1) * D, :]
            grad = nn((mix[h] * nt(d, v)).astype(BF16), k)
            grad = grad + (SCALE * cols[:, 12 + h : 13 + h]) * nt(d, state)
            dq[h] = grad
            dk[h] = nn((mixt[h] * nt(v, d)).astype(BF16), q)
            dv[h] = nn(pairt[h], d)

    acts["ssd"] = ssd_grads
    during("o")

    arrived(total(o_in), o_sem[1])
    scan(o_in, b_out, True)
    b_sem = exchange(lambda chip: b_out.at[chip], lambda sender: b_in.at[own(sender)])
    b_in[own(c), :] = b_out[pl.ds(c, 1)][0]

    def query():
        landed("v")
        inners = []
        for h in range(HH):
            g, k, v, w = head(gb, 0, h), band(kb, h), band(vb, h), wq[h]
            a = nn(w.astype(BF16), v)
            row_inner = jnp.sum(g.astype(F32) * a, axis=-1, keepdims=True)
            inners.append(row_inner)
            put(0, h, a + ssd[h] * root_col)
            gs = (SCALE * w * (nt(g, v) - row_inner)).astype(BF16)
            put(1, h, nn(gs, k) + dq[h])
        stat[0, 16:24, :] = turned_rows(inners)
        send_stat(pl.ds(16, 8), stat_r + 2)
        emit(0, om_ref)
        emit(1, oq_ref)

    def early():
        for dist in (1, 2):
            arrived(stat.at[dist, pl.ds(0, 16)], stat_r + dist - 1)
        landed("q")
        for core_k in range(2):
            line = []
            for dist in range(3):
                here_ok = c + dist < nc
                for core in range(2):
                    off = 2 * dist + core - core_k
                    if 0 <= off < 5:
                        listed = stat[dist, 8 + off : 9 + off, core * D : (core + 1) * D]
                        line.append(jnp.where(here_ok, (1.0 - listed) * BIG, BIG))
                    else:
                        line.append(blank)
            big[core_k : core_k + 1, :] = jnp.concatenate(line, axis=1)
        landed("g")
        for h in range(HH):
            q, g, k = band(qb, h), band(gb, h), head(kb, 2, h)
            peak, inv = [
                jnp.concatenate([stat[n, at : at + 1, :] for n in range(3)], axis=1)
                for at in (h, HH + h)
            ]
            shift = peak + big[0:2, :]
            s = nt(k, q) * SCALE
            w = jnp.exp((s.reshape(2, D, W3) - shift[:, None, :]).reshape(T2, W3)) * inv
            dv[h] = dv[h] + nn(w.astype(BF16), g)
            wk[h] = w

    def late():
        for dist in (1, 2):
            arrived(stat.at[dist, pl.ds(16, 8)], stat_r + 1 + dist)
        for h in range(HH):
            row_inner = jnp.concatenate([stat[n, 16 + h : 17 + h, :] for n in range(3)], axis=1)
            gs = (SCALE * wk[h] * (nt(head(vb, 2, h), band(gb, h)) - row_inner)).astype(BF16)
            dk[h] = dk[h] + nn(gs, band(qb, h))

    acts["query"], acts["early"], acts["late"] = query, early, late
    during("b")

    arrived(b_in.at[pl.ds(0, 512 - part)], b_sem[1])
    def finish(block, store):
        at = pl.ds(pl.multiple_of(block * D, D), D)
        for h in range(HH):
            cut = slice(h * D, (h + 1) * D)
            state = b_in[cut, :]
            weight = cols[at, 8 + h : 9 + h]
            store(2, h, dk[h, at, :] + weight * nt(vb[2, block, :, cut], state))
            store(3, h, dv[h, at, :] + weight * nn(kb[2, block, :, cut], state))

    def for_mate(n, h, value):
        outs[n, 1 - j, :, h * D : (h + 1) * D] = value.astype(BF16)

    def for_here(n, h, value):
        ref = (ok_ref, ov_ref)[n - 2]
        ref[:, pl.ds(pl.multiple_of(j * HW + h * D, D), D)] = value.astype(BF16)

    finish(1 - j, for_mate)
    emit_far(2, ok_ref)
    emit_far(3, ov_ref)
    finish(j, for_here)

    for copy, _ in sends:
        copy.wait_send()
    pltpu.make_async_copy(f_own, f_own, ssem.at[f_sem[0]]).wait()
    for ref, sem in ((l_in, l_sem), (e_out, e_sem), (o_in, o_sem), (b_out, b_sem)):
        pltpu.make_async_copy(total(ref), total(ref), ssem.at[sem[0]]).wait()
    rest_x = xs.at[pl.ds(0, 2 * nx - 1)]
    pltpu.make_async_copy(rest_x, rest_x, ssem.at[x_s]).wait()
    for copy in out_local:
        copy.wait()
    for copy in out_sends:
        copy.wait()


def store(a, b, c, d, ra, rb, rc, rd, sem):
    copies = [
        pltpu.make_async_copy(src, dst, sem.at[n])
        for n, (src, dst) in enumerate(((a, ra), (b, rb), (c, rc), (d, rd)))
    ]
    for copy in copies:
        copy.start()
    for copy in copies:
        copy.wait()


def solution(mesh):
    nc = mesh.shape["ctx"] // 2
    nx = mesh.shape["head"]
    part = 512 // nc

    def body(query_rows, key_rows, value_rows, log_decay, step_size, band_mask, cotangent):
        tok, width = query_rows.shape
        out = jax.ShapeDtypeStruct((tok, width), BF16)
        hbm = pl.BlockSpec(memory_space=pltpu.HBM)
        band = pltpu.VMEM((3, 2, D, HW), BF16)
        tile2 = pltpu.VMEM((2, 8, D), F32)
        share = pltpu.VMEM((nc, part, D), BF16)
        whole = pltpu.VMEM((HW, D), BF16)
        per_head = pltpu.VMEM((HH, T2, D), F32)
        square = pltpu.VMEM((HH, T2, T2), F32)
        results = pl.pallas_call(
            functools.partial(kernel, nc, nx),
            name="mixer",
            out_shape=(pltpu.VMEM((tok, width), BF16),) * 4,
            in_specs=[hbm] * 7,
            out_specs=(pl.BlockSpec(memory_space=pltpu.VMEM),) * 4,
            scratch_shapes=[
                band, band, band, band, pltpu.VMEM((D, HW), BF16), pltpu.VMEM((D, HW), BF16),
                tile2, tile2, tile2, pltpu.VMEM((1, 5), jnp.int32),
                pltpu.VMEM((HW, D), F32), pltpu.VMEM((2, HW, D), F32), pltpu.VMEM((2, nc, 8, D), F32),
                whole, share, share, whole,
                share, whole, share, whole,
                pltpu.VMEM((2 * nx, 8, T2), F32), pltpu.VMEM((3, 24, T2), F32),
                pltpu.VMEM((16, T2), F32), pltpu.VMEM((T2, 16), F32),
                pltpu.VMEM((8, W3), F32), pltpu.VMEM((8, W3), F32),
                square, square, pltpu.VMEM((HH, T2, T2), BF16), pltpu.VMEM((HH, D, T2), BF16),
                per_head, pltpu.VMEM((HH, T2, D), BF16),
                pltpu.VMEM((HH, T2, W3), F32), pltpu.VMEM((HH, T2, W3), F32),
                per_head, per_head, per_head,
                pltpu.VMEM((4, 2, D, HW), BF16),
                pltpu.SemaphoreType.DMA((80,)), pltpu.SemaphoreType.DMA((80,)),
                pltpu.SemaphoreType.DMA((16,)),
            ],
            compiler_params=pltpu.CompilerParams(
                collective_id=0, has_side_effects=True, vmem_limit_bytes=56 << 20
            ),
        )(
            *[
                pltpu.with_memory_space_constraint(a, pltpu.HBM)
                for a in (
                    query_rows, key_rows, value_rows, cotangent, log_decay, step_size, band_mask
                )
            ]
        )
        return pl.pallas_call(
            store,
            name="store",
            out_shape=(out,) * 4,
            in_specs=[pl.BlockSpec(memory_space=pltpu.VMEM)] * 4,
            out_specs=(hbm,) * 4,
            scratch_shapes=[pltpu.SemaphoreType.DMA((4,))],
        )(*[pltpu.with_memory_space_constraint(a, pltpu.VMEM) for a in results])

    return jax.shard_map(
        body,
        mesh=mesh,
        in_specs=(
            P("ctx", "head"),
            P("ctx", "head"),
            P("ctx", "head"),
            P("head", "ctx"),
            P("head", "ctx"),
            P("ctx", None),
            P("ctx", "head"),
        ),
        out_specs=(P("ctx", "head"), P("ctx", "head"), P("ctx", "head"), P("ctx", "head")),
        check_vma=False,
    )
```

```python
import functools

import jax
import jax.numpy as jnp
from jax import lax
from jax.experimental import pallas as pl
from jax.experimental.pallas import tpu as pltpu
from jax.sharding import PartitionSpec as P

MESH = pl.DeviceIdType.MESH
HIGHEST = lax.Precision.HIGHEST
F32 = jnp.float32
BF16 = jnp.bfloat16
D = 128
HH = 4
HW = HH * D
T2 = 256
W3 = 768
CHANNELS = 4096
SCALE = D ** (-0.5)
BIG = 1e30
PLAN = {
    "p": ("k1a", "q1a"),
    "l": ("k1b", "q1b", "v1a", "g1a", "intra"),
    "e": ("v1b", "g1b", "k2a", "q2a", "k2b", "q2b"),
    "x": ("v2a", "g2a"),
    "o": ("v2b", "g2b", "soft", "ssd"),
    "b": ("query", "early", "late"),
}


def nn(a, b):
    return lax.dot_general(a, b, (((1,), (0,)), ((), ())), preferred_element_type=F32)


def nt(a, b):
    return lax.dot_general(a, b, (((1,), (1,)), ((), ())), preferred_element_type=F32)


def tn(a, b):
    return lax.dot_general(a, b, (((0,), (0,)), ((), ())), preferred_element_type=F32)


def kernel(
    nc, nx,
    q_ref, k_ref, v_ref, g_ref, ld_ref, st_ref, bm_ref,
    om_ref, oq_ref, ok_ref, ov_ref,
    kb, vb, qb, gb, kx, vx, ldb, stb, mk, bmv, part_out, part_in, f_in, l_out, l_in, e_out, e_in,
    o_in, o_out, b_out, b_in, xs, stat, rows, cols, bias, big,
    mix, mixt, pairt, qt, ssd, dss, wq, wk, dq, dk, dv, outs,
    ssem, rsem, lsem,
):
    me = lax.axis_index("ctx")
    x = lax.axis_index("head")
    c = me // 2
    j = me % 2
    part = 512 // nc

    def dev(chip, core, xx):
        return (lax.rem(chip, nc) * 2 + core, xx)

    def order(n):
        half = (n + 1) // 2
        return nc // 2 + jnp.where(n % 2 == 0, half, -half)

    barrier = pltpu.get_barrier_semaphore()

    def greet(n, carry):
        pl.semaphore_signal(barrier, 1, device_id=dev(c + order(n), j, x), device_id_type=MESH)
        return carry

    lax.fori_loop(0, nc - 1, greet, 0)
    greeted = nc - 1
    pl.semaphore_signal(barrier, 1, device_id=dev(c, 1 - j, x), device_id_type=MESH)
    greeted += 1
    for step in range(1, nx):
        for core in range(2):
            pl.semaphore_signal(
                barrier, 1, device_id=dev(c, core, lax.rem(x + step, nx)), device_id_type=MESH
            )
            greeted += 1

    sends = []
    count = {"s": 0, "r": 0}

    def slots(kind, n):
        at = count[kind]
        count[kind] += n
        return at

    def remote(src, dst, recv, target):
        copy = pltpu.make_async_remote_copy(
            src_ref=src, dst_ref=dst, send_sem=ssem.at[slots("s", 1)], recv_sem=rsem.at[recv],
            device_id=target, device_id_type=MESH,
        )
        sends.append((copy, src))
        copy.start()

    def arrived(ref, recv):
        pltpu.make_async_copy(ref, ref, rsem.at[recv]).wait()

    def exchange(src_of, dst_of):
        s_at, r_at = slots("s", 1), slots("r", 1)

        def one(n, carry):
            chip = lax.rem(c + order(n), nc)
            pltpu.make_async_remote_copy(
                src_ref=src_of(chip), dst_ref=dst_of(c), send_sem=ssem.at[s_at],
                recv_sem=rsem.at[r_at], device_id=(chip * 2 + j, x), device_id_type=MESH,
            ).start()
            return carry

        lax.fori_loop(0, nc - 1, one, 0, unroll=True)
        return s_at, r_at

    def own(chip):
        return pl.ds(pl.multiple_of(chip * part, part), part)

    def head(ref, slot, h):
        return ref[slot, :, :, h * D : (h + 1) * D].reshape(T2, D)

    def band(ref, h):
        return ref[:, :, :, h * D : (h + 1) * D].reshape(W3, D)

    mine = pl.ds(pl.multiple_of(j * HW, HW), HW)
    other_half = pl.ds(pl.multiple_of((1 - j) * HW, HW), HW)
    local = []
    for n, (src, dst) in enumerate(
        (
            (ld_ref, ldb.at[j]), (st_ref, stb.at[j]), (bm_ref, bmv),
            (k_ref.at[:, mine], kb.at[2, j]), (v_ref.at[:, mine], vb.at[2, j]),
            (k_ref.at[:, other_half], kx), (v_ref.at[:, other_half], vx),
            (q_ref.at[:, mine], qb.at[0, j]), (g_ref.at[:, mine], gb.at[0, j]),
        )
    ):
        copy = pltpu.make_async_copy(src, dst, lsem.at[n])
        copy.start()
        local.append(copy)
    low = j == 0
    at_row = lax.broadcasted_iota(jnp.int32, (T2, T2), 0)
    at_col = lax.broadcasted_iota(jnp.int32, (T2, T2), 1)
    upper = (at_row <= at_col).astype(F32)
    for copy in local[0:3]:
        copy.wait()
    listed = bmv[...].astype(F32)
    mk[j] = jnp.concatenate(
        [jnp.broadcast_to(listed[:, n : n + 1], (1, D)) for n in range(5)]
        + [jnp.zeros((3, D), F32)],
        axis=0,
    )
    own_prefix = lax.dot_general(
        ldb[j], upper[0:D, 0:D], (((1,), (0,)), ((), ())),
        precision=HIGHEST, preferred_element_type=F32,
    )
    own_last = jnp.broadcast_to(own_prefix[:, D - 1 : D], (8, D))
    f_in[pl.ds(j, 1), pl.ds(c, 1)] = own_last[None, None]
    own_carry = jnp.transpose(jnp.exp(own_prefix[:, D - 1 : D] - own_prefix) * stb[j])
    carry_mine = jnp.where(low, own_carry[:, 0:HH], own_carry[:, HH : 2 * HH])
    carry_mate = jnp.where(low, own_carry[:, HH : 2 * HH], own_carry[:, 0:HH])
    for copy in local[3:7]:
        copy.wait()
    for h in range(HH):
        cut = slice(h * D, (h + 1) * D)
        part_out[cut, :] = tn(
            (carry_mate[:, h : h + 1] * kx[:, cut].astype(F32)).astype(BF16), vx[:, cut]
        )
        part_in[j, cut, :] = tn(
            (carry_mine[:, h : h + 1] * kb[2, j, :, cut].astype(F32)).astype(BF16),
            vb[2, j, :, cut],
        )

    pl.semaphore_wait(barrier, greeted)

    mate = dev(c, 1 - j, x)
    small = slots("r", 4)
    remote(ldb.at[j], ldb.at[j], small, mate)
    remote(stb.at[j], stb.at[j], small + 1, mate)
    remote(part_out, part_in.at[j], small + 2, mate)
    remote(mk.at[j], mk.at[j], small + 3, mate)
    f_sem = exchange(lambda chip: f_in.at[j, c], lambda sender: f_in.at[j, sender])
    swap = slots("r", 4)

    def swap_send(n, src, dst, slot):
        remote(src, dst.at[slot, j], swap + n, mate)

    swap_send(0, kx, kb, 2)
    swap_send(1, vx, vb, 2)
    swap_send(2, q_ref.at[:, other_half], qb, 0)
    swap_send(3, g_ref.at[:, other_half], gb, 0)

    first = slots("r", 8)
    second = slots("r", 8)
    ways = {
        "k": (0, k_ref, kb, 2, 0, 1), "v": (1, v_ref, vb, 2, 0, 1),
        "q": (2, q_ref, qb, 0, 2, nc - 1), "g": (3, g_ref, gb, 0, 2, nc - 1),
    }
    swapped = set()

    def have(name):
        n, _, buf, slot, _, _ = ways[name]
        if name not in swapped:
            swapped.add(name)
            arrived(buf.at[slot, 1 - j], swap + n)

    def place(name):
        mates = name[2] == "b"
        at = 2 * ways[name[0]][0] + mates
        return (1 - j if mates else j), first + at, second + at

    def own_on(name):
        _, src, buf, slot, _, step = ways[name[0]]
        block, near, _ = place(name)
        if name[2] == "b":
            have(name[0])
            src = buf.at[slot, block]
        else:
            src = src.at[:, mine]
        remote(src, buf.at[1, block], near, dev(c + step, j, x))

    def hand_on(name):
        _, _, buf, _, far, step = ways[name[0]]
        block, near, later = place(name)
        arrived(buf.at[1, block], near)
        remote(buf.at[1, block], buf.at[far, block], later, dev(c + step, j, x))

    def landed(name):
        _, _, buf, _, far, _ = ways[name]
        for end in "ab":
            block, _, later = place(name + "2" + end)
            arrived(buf.at[far, block], later)

    acts = {}

    def during(window):
        for item in PLAN[window]:
            if item in acts:
                acts[item]()
            elif item[1] == "1":
                own_on(item)
            else:
                hand_on(item)

    during("p")

    arrived(ldb.at[1 - j], small)
    arrived(stb.at[1 - j], small + 1)
    pair = []
    for ref in (ldb, stb):
        wide = jnp.concatenate([ref[0], ref[1]], axis=1)
        pair.append(jnp.where(low, wide[0:HH], wide[HH : 2 * HH]))
    decay, step_row = pair

    fade_late = jnp.exp(jnp.sum(decay[:, D : 2 * D], axis=1, keepdims=True))
    arrived(part_in.at[1 - j], small + 2)
    for h in range(HH):
        cut = slice(h * D, (h + 1) * D)
        l_out[cut, :] = (fade_late[h : h + 1, :] * part_in[0, cut, :] + part_in[1, cut, :]).astype(BF16)
    l_sem = exchange(lambda chip: l_out.at[own(chip)], lambda sender: l_in.at[sender])
    l_in[pl.ds(c, 1)] = l_out[own(c), :][None]

    blank = jnp.full((1, D), BIG, F32)

    def intra():
        prefix = lax.dot_general(
            jnp.concatenate([decay, decay], axis=0), upper, (((1,), (0,)), ((), ())),
            precision=HIGHEST, preferred_element_type=F32,
        )[0:HH]
        last = prefix[:, T2 - 1 : T2]
        carry_row = jnp.exp(last - prefix) * step_row
        packed = jnp.concatenate([prefix, step_row, carry_row, jnp.exp(prefix)], axis=0)
        rows[...] = packed
        cols[...] = jnp.transpose(packed)

        arrived(mk.at[1 - j], small + 3)

        for core in range(2):
            line = []
            for dist in (2, 1, 0):
                for core_k in range(2):
                    off = 2 * dist + core - core_k
                    line.append((1.0 - mk[core, off : off + 1, :]) * BIG if 0 <= off < 5 else blank)
            bias[core : core + 1, :] = jnp.concatenate(line, axis=1) * -1.0

        for copy in local[7:9]:
            copy.wait()
        for name in ways:
            have(name)
        for h in range(HH):
            q, k, v = head(qb, 0, h), head(kb, 2, h), head(vb, 2, h)
            p_row, p_col = rows[h : h + 1, :], cols[:, h : h + 1]
            m = jnp.exp(jnp.where(at_row >= at_col, p_col - p_row, -BIG)) * (
                rows[4 + h : 5 + h, :] * SCALE
            )
            mix[h] = m
            ssd[h] = nn((m * nt(q, k)).astype(BF16), v)
            mt = jnp.exp(jnp.where(at_row <= at_col, p_row - p_col, -BIG)) * (
                cols[:, 4 + h : 5 + h] * SCALE
            )
            mixt[h] = mt
            pairt[h] = (mt * nt(k, q)).astype(BF16)
            qt[h] = jnp.transpose(cols[:, 12 + h : 13 + h] * q.astype(F32)).astype(BF16)

    acts["intra"] = intra
    during("l")

    def total(ref):
        return ref.at[pl.ds(0, nc - 1)]

    row_of = j * HH + c * part // D
    f_mate = slots("r", 1)
    f_own = f_in.at[j, pl.ds(0, nc - 1)]
    arrived(f_own, f_sem[1])
    remote(f_in.at[j], f_in.at[j], f_mate, mate)
    arrived(f_in.at[1 - j], f_mate)
    arrived(total(l_in), l_sem[1])

    def scan(src, dst, reverse):
        def one(n, run):
            chip = nc - 1 - n if reverse else n
            dst[pl.ds(chip, 1)] = run.astype(BF16)[None]
            fade = jnp.exp(
                f_in[0, pl.ds(chip, 1), pl.ds(row_of, 1), :][0]
                + f_in[1, pl.ds(chip, 1), pl.ds(row_of, 1), :][0]
            )
            return fade * run + src[pl.ds(chip, 1)][0].astype(F32)

        lax.fori_loop(0, nc, one, jnp.zeros((part, D), F32), unroll=True)

    scan(l_in, e_out, False)
    e_sem = exchange(lambda chip: e_out.at[chip], lambda sender: e_in.at[own(sender)])
    e_in[own(c), :] = e_out[pl.ds(c, 1)][0]

    during("e")

    rest = e_in.at[pl.ds(0, 512 - part)]
    arrived(rest, e_sem[1])
    squares = jnp.zeros((T2, D), F32)
    inner = jnp.zeros((T2, D), F32)
    for h in range(HH):
        state = e_in[h * D : (h + 1) * D, :]
        y = ssd[h] + (SCALE * cols[:, 12 + h : 13 + h]) * nn(head(qb, 0, h), state)
        ssd[h] = y
        squares = squares + y * y
        inner = inner + y * head(gb, 0, h).astype(F32)
    ones = jnp.ones((8, D), BF16)

    def across(a):
        head_part = a.astype(BF16)
        return nt(ones, head_part) + nt(ones, (a - head_part.astype(F32)).astype(BF16))

    sums = jnp.concatenate([across(squares)[0:4], across(inner)[0:4]], axis=0)
    here = x * 2 + j
    xs[pl.ds(here, 1)] = sums[None]
    x_s, x_r = slots("s", 1), slots("r", 1)
    for step in range(nx):
        for core in range(2):
            if step == 0 and core == 0:
                continue
            pltpu.make_async_remote_copy(
                src_ref=xs.at[here], dst_ref=xs.at[here], send_sem=ssem.at[x_s],
                recv_sem=rsem.at[x_r],
                device_id=dev(c, (j + core) % 2, lax.rem(x + step, nx)), device_id_type=MESH,
            ).start()

    columns = []

    def turned_rows(kinds):
        lane = lax.broadcasted_iota(jnp.int32, (T2, D), 1)
        grid = jnp.zeros((T2, D), F32)
        for n, column in enumerate(kinds):
            grid = jnp.where(lane == n, column, grid)
        return jnp.transpose(grid)[0:8]

    def send_stat(lines, at):
        for dist in (1, 2):
            remote(
                stat.at[0, lines], stat.at[dist, lines], at + dist - 1, dev(c + nc - dist, j, x)
            )

    stat_r = slots("r", 4)

    def soft():
        landed("k")
        for h in range(HH):
            s = nt(head(qb, 0, h), band(kb, h)) * SCALE
            s = (s.reshape(2, D, W3) + bias[0:2, :][:, None, :]).reshape(T2, W3)
            peak = jnp.max(s, axis=-1, keepdims=True)
            e = jnp.exp(s - peak)
            inv = 1.0 / jnp.sum(e, axis=-1, keepdims=True)
            wq[h] = e * inv
            columns.append((peak, inv))
        stat[0, 0:8, :] = turned_rows([p for p, _ in columns] + [i for _, i in columns])
        stat[0, 8:16, :] = jnp.concatenate([mk[0], mk[1]], axis=1)
        send_stat(pl.ds(0, 16), stat_r)

    acts["soft"] = soft
    during("x")

    arrived(xs.at[pl.ds(0, 2 * nx - 1)], x_r)
    both = xs[0]
    for n in range(1, 2 * nx):
        both = both + xs[n]
    inv_root = 1.0 / jnp.sqrt(both[0:4] / CHANNELS + 1e-05)
    cross = both[4:8] * inv_root / CHANNELS
    turned = jnp.transpose(jnp.concatenate([inv_root, inv_root * inv_root * cross], axis=0))
    root_col, slope_col = turned[:, 0:1], turned[:, 4:5]
    for h in range(HH):
        g = head(gb, 0, h).astype(F32)
        y = ssd[h]
        d = (g * root_col - y * slope_col).astype(BF16)
        dss[h] = d
        o_out[h * D : (h + 1) * D, :] = (SCALE * nn(qt[h], d)).astype(BF16)
    o_in[pl.ds(c, 1)] = o_out[own(c), :][None]
    o_sem = exchange(lambda chip: o_out.at[own(chip)], lambda sender: o_in.at[sender])

    out_sends = []
    out_local = []
    out_r = slots("r", 4)

    def emit(n, ref):
        copy = pltpu.make_async_copy(outs.at[n, j], ref.at[:, mine], lsem.at[9 + n])
        copy.start()
        out_local.append(copy)
        emit_far(n, ref)

    def emit_far(n, ref):
        far = pltpu.make_async_remote_copy(
            src_ref=outs.at[n, 1 - j], dst_ref=ref.at[:, mine], send_sem=ssem.at[slots("s", 1)],
            recv_sem=rsem.at[out_r + n], device_id=mate, device_id_type=MESH,
        )
        far.start()
        out_sends.append(far)

    def put(n, h, value):
        outs[n, :, :, h * D : (h + 1) * D] = value.astype(BF16).reshape(2, D, D)

    def ssd_grads():
        for h in range(HH):
            q, k, v, d = head(qb, 0, h), head(kb, 2, h), head(vb, 2, h), dss[h]
            state = e_in[h * D : (h + 1) * D, :]
            grad = nn((mix[h] * nt(d, v)).astype(BF16), k)
            grad = grad + (SCALE * cols[:, 12 + h : 13 + h]) * nt(d, state)
            dq[h] = grad
            dk[h] = nn((mixt[h] * nt(v, d)).astype(BF16), q)
            dv[h] = nn(pairt[h], d)

    acts["ssd"] = ssd_grads
    during("o")

    arrived(total(o_in), o_sem[1])
    scan(o_in, b_out, True)
    b_sem = exchange(lambda chip: b_out.at[chip], lambda sender: b_in.at[own(sender)])
    b_in[own(c), :] = b_out[pl.ds(c, 1)][0]

    def query():
        landed("v")
        inners = []
        for h in range(HH):
            g, k, v, w = head(gb, 0, h), band(kb, h), band(vb, h), wq[h]
            a = nn(w.astype(BF16), v)
            row_inner = jnp.sum(g.astype(F32) * a, axis=-1, keepdims=True)
            inners.append(row_inner)
            put(0, h, a + ssd[h] * root_col)
            gs = (SCALE * w * (nt(g, v) - row_inner)).astype(BF16)
            put(1, h, nn(gs, k) + dq[h])
        stat[0, 16:24, :] = turned_rows(inners)
        send_stat(pl.ds(16, 8), stat_r + 2)
        emit(0, om_ref)
        emit(1, oq_ref)

    def early():
        for dist in (1, 2):
            arrived(stat.at[dist, pl.ds(0, 16)], stat_r + dist - 1)
        landed("q")
        for core_k in range(2):
            line = []
            for dist in range(3):
                here_ok = c + dist < nc
                for core in range(2):
                    off = 2 * dist + core - core_k
                    if 0 <= off < 5:
                        listed = stat[dist, 8 + off : 9 + off, core * D : (core + 1) * D]
                        line.append(jnp.where(here_ok, (1.0 - listed) * BIG, BIG))
                    else:
                        line.append(blank)
            big[core_k : core_k + 1, :] = jnp.concatenate(line, axis=1)
        landed("g")
        for h in range(HH):
            q, g, k = band(qb, h), band(gb, h), head(kb, 2, h)
            peak, inv = [
                jnp.concatenate([stat[n, at : at + 1, :] for n in range(3)], axis=1)
                for at in (h, HH + h)
            ]
            shift = peak + big[0:2, :]
            s = nt(k, q) * SCALE
            w = jnp.exp((s.reshape(2, D, W3) - shift[:, None, :]).reshape(T2, W3)) * inv
            dv[h] = dv[h] + nn(w.astype(BF16), g)
            wk[h] = w

    def late():
        for dist in (1, 2):
            arrived(stat.at[dist, pl.ds(16, 8)], stat_r + 1 + dist)
        for h in range(HH):
            row_inner = jnp.concatenate([stat[n, 16 + h : 17 + h, :] for n in range(3)], axis=1)
            gs = (SCALE * wk[h] * (nt(head(vb, 2, h), band(gb, h)) - row_inner)).astype(BF16)
            dk[h] = dk[h] + nn(gs, band(qb, h))

    acts["query"], acts["early"], acts["late"] = query, early, late
    during("b")

    arrived(b_in.at[pl.ds(0, 512 - part)], b_sem[1])
    def finish(block, store):
        at = pl.ds(pl.multiple_of(block * D, D), D)
        for h in range(HH):
            cut = slice(h * D, (h + 1) * D)
            state = b_in[cut, :]
            weight = cols[at, 8 + h : 9 + h]
            store(2, h, dk[h, at, :] + weight * nt(vb[2, block, :, cut], state))
            store(3, h, dv[h, at, :] + weight * nn(kb[2, block, :, cut], state))

    def for_mate(n, h, value):
        outs[n, 1 - j, :, h * D : (h + 1) * D] = value.astype(BF16)

    def for_here(n, h, value):
        ref = (ok_ref, ov_ref)[n - 2]
        ref[:, pl.ds(pl.multiple_of(j * HW + h * D, D), D)] = value.astype(BF16)

    finish(1 - j, for_mate)
    emit_far(2, ok_ref)
    emit_far(3, ov_ref)
    finish(j, for_here)

    for copy, _ in sends:
        copy.wait_send()
    pltpu.make_async_copy(f_own, f_own, ssem.at[f_sem[0]]).wait()
    for ref, sem in ((l_in, l_sem), (e_out, e_sem), (o_in, o_sem), (b_out, b_sem)):
        pltpu.make_async_copy(total(ref), total(ref), ssem.at[sem[0]]).wait()
    rest_x = xs.at[pl.ds(0, 2 * nx - 1)]
    pltpu.make_async_copy(rest_x, rest_x, ssem.at[x_s]).wait()
    for copy in out_local:
        copy.wait()
    for copy in out_sends:
        copy.wait()


def store(a, b, c, d, ra, rb, rc, rd, sem):
    copies = [
        pltpu.make_async_copy(src, dst, sem.at[n])
        for n, (src, dst) in enumerate(((a, ra), (b, rb), (c, rc), (d, rd)))
    ]
    for copy in copies:
        copy.start()
    for copy in copies:
        copy.wait()


def solution(mesh):
    nc = mesh.shape["ctx"] // 2
    nx = mesh.shape["head"]
    part = 512 // nc

    def body(query_rows, key_rows, value_rows, log_decay, step_size, band_mask, cotangent):
        tok, width = query_rows.shape
        out = jax.ShapeDtypeStruct((tok, width), BF16)
        hbm = pl.BlockSpec(memory_space=pltpu.HBM)
        band = pltpu.VMEM((3, 2, D, HW), BF16)
        tile2 = pltpu.VMEM((2, 8, D), F32)
        share = pltpu.VMEM((nc, part, D), BF16)
        whole = pltpu.VMEM((HW, D), BF16)
        per_head = pltpu.VMEM((HH, T2, D), F32)
        square = pltpu.VMEM((HH, T2, T2), F32)
        results = pl.pallas_call(
            functools.partial(kernel, nc, nx),
            name="mixer",
            out_shape=(pltpu.VMEM((tok, width), BF16),) * 4,
            in_specs=[hbm] * 7,
            out_specs=(pl.BlockSpec(memory_space=pltpu.VMEM),) * 4,
            scratch_shapes=[
                band, band, band, band, pltpu.VMEM((D, HW), BF16), pltpu.VMEM((D, HW), BF16),
                tile2, tile2, tile2, pltpu.VMEM((1, 5), jnp.int32),
                pltpu.VMEM((HW, D), F32), pltpu.VMEM((2, HW, D), F32), pltpu.VMEM((2, nc, 8, D), F32),
                whole, share, share, whole,
                share, whole, share, whole,
                pltpu.VMEM((2 * nx, 8, T2), F32), pltpu.VMEM((3, 24, T2), F32),
                pltpu.VMEM((16, T2), F32), pltpu.VMEM((T2, 16), F32),
                pltpu.VMEM((8, W3), F32), pltpu.VMEM((8, W3), F32),
                square, square, pltpu.VMEM((HH, T2, T2), BF16), pltpu.VMEM((HH, D, T2), BF16),
                per_head, pltpu.VMEM((HH, T2, D), BF16),
                pltpu.VMEM((HH, T2, W3), F32), pltpu.VMEM((HH, T2, W3), F32),
                per_head, per_head, per_head,
                pltpu.VMEM((4, 2, D, HW), BF16),
                pltpu.SemaphoreType.DMA((80,)), pltpu.SemaphoreType.DMA((80,)),
                pltpu.SemaphoreType.DMA((16,)),
            ],
            compiler_params=pltpu.CompilerParams(
                collective_id=0, has_side_effects=True, vmem_limit_bytes=56 << 20
            ),
        )(
            *[
                pltpu.with_memory_space_constraint(a, pltpu.HBM)
                for a in (
                    query_rows, key_rows, value_rows, cotangent, log_decay, step_size, band_mask
                )
            ]
        )
        return pl.pallas_call(
            store,
            name="store",
            out_shape=(out,) * 4,
            in_specs=[pl.BlockSpec(memory_space=pltpu.VMEM)] * 4,
            out_specs=(hbm,) * 4,
            scratch_shapes=[pltpu.SemaphoreType.DMA((4,))],
        )(*[pltpu.with_memory_space_constraint(a, pltpu.VMEM) for a in results])

    return jax.shard_map(
        body,
        mesh=mesh,
        in_specs=(
            P("ctx", "head"),
            P("ctx", "head"),
            P("ctx", "head"),
            P("head", "ctx"),
            P("head", "ctx"),
            P("ctx", None),
            P("ctx", "head"),
        ),
        out_specs=(P("ctx", "head"), P("ctx", "head"), P("ctx", "head"), P("ctx", "head")),
        check_vma=False,
    )
```

```python
import functools

import jax
import jax.numpy as jnp
from jax import lax
from jax.experimental import pallas as pl
from jax.experimental.pallas import tpu as pltpu
from jax.sharding import PartitionSpec as P

MESH = pl.DeviceIdType.MESH
HIGHEST = lax.Precision.HIGHEST
F32 = jnp.float32
BF16 = jnp.bfloat16
D = 128
HH = 4
HW = HH * D
T2 = 256
W3 = 768
CHANNELS = 4096
SCALE = D ** (-0.5)
BIG = 1e30
PLAN = {
    "p": ("k1a", "q1a"),
    "l": ("k1b", "q1b", "v1a", "g1a", "intra"),
    "e": ("v1b", "g1b", "k2a", "q2a", "k2b", "q2b"),
    "x": ("v2a", "g2a"),
    "o": ("v2b", "g2b", "soft", "ssd"),
    "b": ("query", "early", "late"),
}


def nn(a, b):
    return lax.dot_general(a, b, (((1,), (0,)), ((), ())), preferred_element_type=F32)


def nt(a, b):
    return lax.dot_general(a, b, (((1,), (1,)), ((), ())), preferred_element_type=F32)


def tn(a, b):
    return lax.dot_general(a, b, (((0,), (0,)), ((), ())), preferred_element_type=F32)


def kernel(
    nc, nx,
    q_ref, k_ref, v_ref, g_ref, ld_ref, st_ref, bm_ref,
    om_ref, oq_ref, ok_ref, ov_ref,
    kb, vb, qb, gb, kx, vx, ldb, stb, mk, bmv, part_out, part_in, part_own, f_in, l_out, l_in, e_out, e_in,
    o_in, o_out, b_out, b_in, xs, stat, rows, cols, bias, big,
    mix, mixt, pairt, qt, ssd, dss, wq, wk, dq, dk, dv, outs,
    ssem, rsem, lsem,
):
    me = lax.axis_index("ctx")
    x = lax.axis_index("head")
    c = me // 2
    j = me % 2
    part = 512 // nc

    def dev(chip, core, xx):
        return (lax.rem(chip, nc) * 2 + core, xx)

    def order(n):
        half = (n + 1) // 2
        return nc // 2 + jnp.where(n % 2 == 0, half, -half)

    barrier = pltpu.get_barrier_semaphore()

    def greet(n, carry):
        pl.semaphore_signal(barrier, 1, device_id=dev(c + order(n), j, x), device_id_type=MESH)
        return carry

    lax.fori_loop(0, nc - 1, greet, 0)
    greeted = nc - 1
    pl.semaphore_signal(barrier, 1, device_id=dev(c, 1 - j, x), device_id_type=MESH)
    greeted += 1
    for step in range(1, nx):
        for core in range(2):
            pl.semaphore_signal(
                barrier, 1, device_id=dev(c, core, lax.rem(x + step, nx)), device_id_type=MESH
            )
            greeted += 1

    sends = []
    count = {"s": 0, "r": 0}

    def slots(kind, n):
        at = count[kind]
        count[kind] += n
        return at

    def remote(src, dst, recv, target):
        copy = pltpu.make_async_remote_copy(
            src_ref=src, dst_ref=dst, send_sem=ssem.at[slots("s", 1)], recv_sem=rsem.at[recv],
            device_id=target, device_id_type=MESH,
        )
        sends.append((copy, src))
        copy.start()

    def arrived(ref, recv):
        pltpu.make_async_copy(ref, ref, rsem.at[recv]).wait()

    def exchange(src_of, dst_of):
        s_at, r_at = slots("s", 1), slots("r", 1)

        def one(n, carry):
            chip = lax.rem(c + order(n), nc)
            pltpu.make_async_remote_copy(
                src_ref=src_of(chip), dst_ref=dst_of(c), send_sem=ssem.at[s_at],
                recv_sem=rsem.at[r_at], device_id=(chip * 2 + j, x), device_id_type=MESH,
            ).start()
            return carry

        lax.fori_loop(0, nc - 1, one, 0, unroll=True)
        return s_at, r_at

    def own(chip):
        return pl.ds(pl.multiple_of(chip * part, part), part)

    def head(ref, slot, h):
        return ref[slot, :, :, h * D : (h + 1) * D].reshape(T2, D)

    def band(ref, h):
        return ref[:, :, :, h * D : (h + 1) * D].reshape(W3, D)

    mine = pl.ds(pl.multiple_of(j * HW, HW), HW)
    other_half = pl.ds(pl.multiple_of((1 - j) * HW, HW), HW)
    local = []
    for n, (src, dst) in enumerate(
        (
            (ld_ref, ldb.at[j]), (st_ref, stb.at[j]), (bm_ref, bmv),
            (k_ref.at[:, mine], kb.at[2, j]), (v_ref.at[:, mine], vb.at[2, j]),
            (k_ref.at[:, other_half], kx), (v_ref.at[:, other_half], vx),
            (q_ref.at[:, mine], qb.at[0, j]), (g_ref.at[:, mine], gb.at[0, j]),
        )
    ):
        copy = pltpu.make_async_copy(src, dst, lsem.at[n])
        copy.start()
        local.append(copy)
    low = j == 0
    at_row = lax.broadcasted_iota(jnp.int32, (T2, T2), 0)
    at_col = lax.broadcasted_iota(jnp.int32, (T2, T2), 1)
    upper = (at_row <= at_col).astype(F32)
    for copy in local[0:3]:
        copy.wait()
    listed = bmv[...].astype(F32)
    mk[j] = jnp.concatenate(
        [jnp.broadcast_to(listed[:, n : n + 1], (1, D)) for n in range(5)]
        + [jnp.zeros((3, D), F32)],
        axis=0,
    )
    own_prefix = lax.dot_general(
        ldb[j], upper[0:D, 0:D], (((1,), (0,)), ((), ())),
        precision=HIGHEST, preferred_element_type=F32,
    )
    own_last = jnp.broadcast_to(own_prefix[:, D - 1 : D], (8, D))
    f_in[pl.ds(j, 1), pl.ds(c, 1)] = own_last[None, None]
    own_carry = jnp.transpose(jnp.exp(own_prefix[:, D - 1 : D] - own_prefix) * stb[j])
    carry_mine = jnp.where(low, own_carry[:, 0:HH], own_carry[:, HH : 2 * HH])
    carry_mate = jnp.where(low, own_carry[:, HH : 2 * HH], own_carry[:, 0:HH])
    for copy in local[3:7]:
        copy.wait()
    for h in range(HH):
        cut = slice(h * D, (h + 1) * D)
        part_out[cut, :] = tn(
            (carry_mate[:, h : h + 1] * kx[:, cut].astype(F32)).astype(BF16), vx[:, cut]
        ).astype(BF16)
        part_own[cut, :] = tn(
            (carry_mine[:, h : h + 1] * kb[2, j, :, cut].astype(F32)).astype(BF16),
            vb[2, j, :, cut],
        )

    pl.semaphore_wait(barrier, greeted)

    mate = dev(c, 1 - j, x)
    small = slots("r", 4)
    remote(ldb.at[j], ldb.at[j], small, mate)
    remote(stb.at[j], stb.at[j], small + 1, mate)
    remote(part_out, part_in, small + 2, mate)
    remote(mk.at[j], mk.at[j], small + 3, mate)
    f_sem = exchange(lambda chip: f_in.at[j, c], lambda sender: f_in.at[j, sender])
    swap = slots("r", 4)

    def swap_send(n, src, dst, slot):
        remote(src, dst.at[slot, j], swap + n, mate)

    swap_send(0, kx, kb, 2)
    swap_send(1, vx, vb, 2)
    swap_send(2, q_ref.at[:, other_half], qb, 0)
    swap_send(3, g_ref.at[:, other_half], gb, 0)

    first = slots("r", 8)
    second = slots("r", 8)
    ways = {
        "k": (0, k_ref, kb, 2, 0, 1), "v": (1, v_ref, vb, 2, 0, 1),
        "q": (2, q_ref, qb, 0, 2, nc - 1), "g": (3, g_ref, gb, 0, 2, nc - 1),
    }
    swapped = set()

    def have(name):
        n, _, buf, slot, _, _ = ways[name]
        if name not in swapped:
            swapped.add(name)
            arrived(buf.at[slot, 1 - j], swap + n)

    def place(name):
        mates = name[2] == "b"
        at = 2 * ways[name[0]][0] + mates
        return (1 - j if mates else j), first + at, second + at

    def own_on(name):
        _, src, buf, slot, _, step = ways[name[0]]
        block, near, _ = place(name)
        if name[2] == "b":
            have(name[0])
            src = buf.at[slot, block]
        else:
            src = src.at[:, mine]
        remote(src, buf.at[1, block], near, dev(c + step, j, x))

    def hand_on(name):
        _, _, buf, _, far, step = ways[name[0]]
        block, near, later = place(name)
        arrived(buf.at[1, block], near)
        remote(buf.at[1, block], buf.at[far, block], later, dev(c + step, j, x))

    def landed(name):
        _, _, buf, _, far, _ = ways[name]
        for end in "ab":
            block, _, later = place(name + "2" + end)
            arrived(buf.at[far, block], later)

    acts = {}

    def during(window):
        for item in PLAN[window]:
            if item in acts:
                acts[item]()
            elif item[1] == "1":
                own_on(item)
            else:
                hand_on(item)

    during("p")

    arrived(ldb.at[1 - j], small)
    arrived(stb.at[1 - j], small + 1)
    pair = []
    for ref in (ldb, stb):
        wide = jnp.concatenate([ref[0], ref[1]], axis=1)
        pair.append(jnp.where(low, wide[0:HH], wide[HH : 2 * HH]))
    decay, step_row = pair

    fade_late = jnp.exp(jnp.sum(decay[:, D : 2 * D], axis=1, keepdims=True))
    arrived(part_in, small + 2)
    of_own, of_mate = jnp.where(low, fade_late, 1.0), jnp.where(low, 1.0, fade_late)
    for h in range(HH):
        cut = slice(h * D, (h + 1) * D)
        l_out[cut, :] = (
            of_own[h : h + 1, :] * part_own[cut, :]
            + of_mate[h : h + 1, :] * part_in[cut, :].astype(F32)
        ).astype(BF16)
    l_sem = exchange(lambda chip: l_out.at[own(chip)], lambda sender: l_in.at[sender])
    l_in[pl.ds(c, 1)] = l_out[own(c), :][None]

    blank = jnp.full((1, D), BIG, F32)

    def intra():
        prefix = lax.dot_general(
            jnp.concatenate([decay, decay], axis=0), upper, (((1,), (0,)), ((), ())),
            precision=HIGHEST, preferred_element_type=F32,
        )[0:HH]
        last = prefix[:, T2 - 1 : T2]
        carry_row = jnp.exp(last - prefix) * step_row
        packed = jnp.concatenate([prefix, step_row, carry_row, jnp.exp(prefix)], axis=0)
        rows[...] = packed
        cols[...] = jnp.transpose(packed)

        arrived(mk.at[1 - j], small + 3)

        for core in range(2):
            line = []
            for dist in (2, 1, 0):
                for core_k in range(2):
                    off = 2 * dist + core - core_k
                    line.append((1.0 - mk[core, off : off + 1, :]) * BIG if 0 <= off < 5 else blank)
            bias[core : core + 1, :] = jnp.concatenate(line, axis=1) * -1.0

        for copy in local[7:9]:
            copy.wait()
        for name in ways:
            have(name)
        for h in range(HH):
            q, k, v = head(qb, 0, h), head(kb, 2, h), head(vb, 2, h)
            p_row, p_col = rows[h : h + 1, :], cols[:, h : h + 1]
            m = jnp.exp(jnp.where(at_row >= at_col, p_col - p_row, -BIG)) * (
                rows[4 + h : 5 + h, :] * SCALE
            )
            mix[h] = m
            ssd[h] = nn((m * nt(q, k)).astype(BF16), v)
            mt = jnp.exp(jnp.where(at_row <= at_col, p_row - p_col, -BIG)) * (
                cols[:, 4 + h : 5 + h] * SCALE
            )
            mixt[h] = mt
            pairt[h] = (mt * nt(k, q)).astype(BF16)
            qt[h] = jnp.transpose(cols[:, 12 + h : 13 + h] * q.astype(F32)).astype(BF16)

    acts["intra"] = intra
    during("l")

    def total(ref):
        return ref.at[pl.ds(0, nc - 1)]

    row_of = j * HH + c * part // D
    f_mate = slots("r", 1)
    f_own = f_in.at[j, pl.ds(0, nc - 1)]
    arrived(f_own, f_sem[1])
    remote(f_in.at[j], f_in.at[j], f_mate, mate)
    arrived(f_in.at[1 - j], f_mate)
    arrived(total(l_in), l_sem[1])

    def scan(src, dst, reverse):
        def one(n, run):
            chip = nc - 1 - n if reverse else n
            dst[pl.ds(chip, 1)] = run.astype(BF16)[None]
            fade = jnp.exp(
                f_in[0, pl.ds(chip, 1), pl.ds(row_of, 1), :][0]
                + f_in[1, pl.ds(chip, 1), pl.ds(row_of, 1), :][0]
            )
            return fade * run + src[pl.ds(chip, 1)][0].astype(F32)

        lax.fori_loop(0, nc, one, jnp.zeros((part, D), F32), unroll=True)

    scan(l_in, e_out, False)
    e_sem = exchange(lambda chip: e_out.at[chip], lambda sender: e_in.at[own(sender)])
    e_in[own(c), :] = e_out[pl.ds(c, 1)][0]

    during("e")

    rest = e_in.at[pl.ds(0, 512 - part)]
    arrived(rest, e_sem[1])
    squares = jnp.zeros((T2, D), F32)
    inner = jnp.zeros((T2, D), F32)
    for h in range(HH):
        state = e_in[h * D : (h + 1) * D, :]
        y = ssd[h] + (SCALE * cols[:, 12 + h : 13 + h]) * nn(head(qb, 0, h), state)
        ssd[h] = y
        squares = squares + y * y
        inner = inner + y * head(gb, 0, h).astype(F32)
    ones = jnp.ones((8, D), BF16)

    def across(a):
        head_part = a.astype(BF16)
        return nt(ones, head_part) + nt(ones, (a - head_part.astype(F32)).astype(BF16))

    sums = jnp.concatenate([across(squares)[0:4], across(inner)[0:4]], axis=0)
    here = x * 2 + j
    xs[pl.ds(here, 1)] = sums[None]
    x_s, x_r = slots("s", 1), slots("r", 1)
    for step in range(nx):
        for core in range(2):
            if step == 0 and core == 0:
                continue
            pltpu.make_async_remote_copy(
                src_ref=xs.at[here], dst_ref=xs.at[here], send_sem=ssem.at[x_s],
                recv_sem=rsem.at[x_r],
                device_id=dev(c, (j + core) % 2, lax.rem(x + step, nx)), device_id_type=MESH,
            ).start()

    columns = []

    def turned_rows(kinds):
        lane = lax.broadcasted_iota(jnp.int32, (T2, D), 1)
        grid = jnp.zeros((T2, D), F32)
        for n, column in enumerate(kinds):
            grid = jnp.where(lane == n, column, grid)
        return jnp.transpose(grid)[0:8]

    def send_stat(lines, at):
        for dist in (1, 2):
            remote(
                stat.at[0, lines], stat.at[dist, lines], at + dist - 1, dev(c + nc - dist, j, x)
            )

    stat_r = slots("r", 4)

    def soft():
        landed("k")
        for h in range(HH):
            s = nt(head(qb, 0, h), band(kb, h)) * SCALE
            s = (s.reshape(2, D, W3) + bias[0:2, :][:, None, :]).reshape(T2, W3)
            peak = jnp.max(s, axis=-1, keepdims=True)
            e = jnp.exp(s - peak)
            inv = 1.0 / jnp.sum(e, axis=-1, keepdims=True)
            wq[h] = e * inv
            columns.append((peak, inv))
        stat[0, 0:8, :] = turned_rows([p for p, _ in columns] + [i for _, i in columns])
        stat[0, 8:16, :] = jnp.concatenate([mk[0], mk[1]], axis=1)
        send_stat(pl.ds(0, 16), stat_r)

    acts["soft"] = soft
    during("x")

    arrived(xs.at[pl.ds(0, 2 * nx - 1)], x_r)
    both = xs[0]
    for n in range(1, 2 * nx):
        both = both + xs[n]
    inv_root = 1.0 / jnp.sqrt(both[0:4] / CHANNELS + 1e-05)
    cross = both[4:8] * inv_root / CHANNELS
    turned = jnp.transpose(jnp.concatenate([inv_root, inv_root * inv_root * cross], axis=0))
    root_col, slope_col = turned[:, 0:1], turned[:, 4:5]
    for h in range(HH):
        g = head(gb, 0, h).astype(F32)
        y = ssd[h]
        d = (g * root_col - y * slope_col).astype(BF16)
        dss[h] = d
        o_out[h * D : (h + 1) * D, :] = (SCALE * nn(qt[h], d)).astype(BF16)
    o_in[pl.ds(c, 1)] = o_out[own(c), :][None]
    o_sem = exchange(lambda chip: o_out.at[own(chip)], lambda sender: o_in.at[sender])

    out_sends = []
    out_local = []
    out_r = slots("r", 4)

    def emit(n, ref):
        copy = pltpu.make_async_copy(outs.at[n, j], ref.at[:, mine], lsem.at[9 + n])
        copy.start()
        out_local.append(copy)
        emit_far(n, ref)

    def emit_far(n, ref):
        far = pltpu.make_async_remote_copy(
            src_ref=outs.at[n, 1 - j], dst_ref=ref.at[:, mine], send_sem=ssem.at[slots("s", 1)],
            recv_sem=rsem.at[out_r + n], device_id=mate, device_id_type=MESH,
        )
        far.start()
        out_sends.append(far)

    def put(n, h, value):
        outs[n, :, :, h * D : (h + 1) * D] = value.astype(BF16).reshape(2, D, D)

    def ssd_grads():
        for h in range(HH):
            q, k, v, d = head(qb, 0, h), head(kb, 2, h), head(vb, 2, h), dss[h]
            state = e_in[h * D : (h + 1) * D, :]
            grad = nn((mix[h] * nt(d, v)).astype(BF16), k)
            grad = grad + (SCALE * cols[:, 12 + h : 13 + h]) * nt(d, state)
            dq[h] = grad
            dk[h] = nn((mixt[h] * nt(v, d)).astype(BF16), q)
            dv[h] = nn(pairt[h], d)

    acts["ssd"] = ssd_grads
    during("o")

    arrived(total(o_in), o_sem[1])
    scan(o_in, b_out, True)
    b_sem = exchange(lambda chip: b_out.at[chip], lambda sender: b_in.at[own(sender)])
    b_in[own(c), :] = b_out[pl.ds(c, 1)][0]

    def query():
        landed("v")
        inners = []
        for h in range(HH):
            g, k, v, w = head(gb, 0, h), band(kb, h), band(vb, h), wq[h]
            a = nn(w.astype(BF16), v)
            row_inner = jnp.sum(g.astype(F32) * a, axis=-1, keepdims=True)
            inners.append(row_inner)
            put(0, h, a + ssd[h] * root_col)
            gs = (SCALE * w * (nt(g, v) - row_inner)).astype(BF16)
            put(1, h, nn(gs, k) + dq[h])
        stat[0, 16:24, :] = turned_rows(inners)
        send_stat(pl.ds(16, 8), stat_r + 2)
        emit(0, om_ref)
        emit(1, oq_ref)

    def early():
        for dist in (1, 2):
            arrived(stat.at[dist, pl.ds(0, 16)], stat_r + dist - 1)
        landed("q")
        for core_k in range(2):
            line = []
            for dist in range(3):
                here_ok = c + dist < nc
                for core in range(2):
                    off = 2 * dist + core - core_k
                    if 0 <= off < 5:
                        listed = stat[dist, 8 + off : 9 + off, core * D : (core + 1) * D]
                        line.append(jnp.where(here_ok, (1.0 - listed) * BIG, BIG))
                    else:
                        line.append(blank)
            big[core_k : core_k + 1, :] = jnp.concatenate(line, axis=1)
        landed("g")
        for h in range(HH):
            q, g, k = band(qb, h), band(gb, h), head(kb, 2, h)
            peak, inv = [
                jnp.concatenate([stat[n, at : at + 1, :] for n in range(3)], axis=1)
                for at in (h, HH + h)
            ]
            shift = peak + big[0:2, :]
            s = nt(k, q) * SCALE
            w = jnp.exp((s.reshape(2, D, W3) - shift[:, None, :]).reshape(T2, W3)) * inv
            dv[h] = dv[h] + nn(w.astype(BF16), g)
            wk[h] = w

    def late():
        for dist in (1, 2):
            arrived(stat.at[dist, pl.ds(16, 8)], stat_r + 1 + dist)
        for h in range(HH):
            row_inner = jnp.concatenate([stat[n, 16 + h : 17 + h, :] for n in range(3)], axis=1)
            gs = (SCALE * wk[h] * (nt(head(vb, 2, h), band(gb, h)) - row_inner)).astype(BF16)
            dk[h] = dk[h] + nn(gs, band(qb, h))

    acts["query"], acts["early"], acts["late"] = query, early, late
    during("b")

    arrived(b_in.at[pl.ds(0, 512 - part)], b_sem[1])
    def finish(block, store):
        at = pl.ds(pl.multiple_of(block * D, D), D)
        for h in range(HH):
            cut = slice(h * D, (h + 1) * D)
            state = b_in[cut, :]
            weight = cols[at, 8 + h : 9 + h]
            store(2, h, dk[h, at, :] + weight * nt(vb[2, block, :, cut], state))
            store(3, h, dv[h, at, :] + weight * nn(kb[2, block, :, cut], state))

    def for_mate(n, h, value):
        outs[n, 1 - j, :, h * D : (h + 1) * D] = value.astype(BF16)

    def for_here(n, h, value):
        ref = (ok_ref, ov_ref)[n - 2]
        ref[:, pl.ds(pl.multiple_of(j * HW + h * D, D), D)] = value.astype(BF16)

    finish(1 - j, for_mate)
    emit_far(2, ok_ref)
    emit_far(3, ov_ref)
    finish(j, for_here)

    for copy, _ in sends:
        copy.wait_send()
    pltpu.make_async_copy(f_own, f_own, ssem.at[f_sem[0]]).wait()
    for ref, sem in ((l_in, l_sem), (e_out, e_sem), (o_in, o_sem), (b_out, b_sem)):
        pltpu.make_async_copy(total(ref), total(ref), ssem.at[sem[0]]).wait()
    rest_x = xs.at[pl.ds(0, 2 * nx - 1)]
    pltpu.make_async_copy(rest_x, rest_x, ssem.at[x_s]).wait()
    for copy in out_local:
        copy.wait()
    for copy in out_sends:
        copy.wait()


def store(a, b, c, d, ra, rb, rc, rd, sem):
    copies = [
        pltpu.make_async_copy(src, dst, sem.at[n])
        for n, (src, dst) in enumerate(((a, ra), (b, rb), (c, rc), (d, rd)))
    ]
    for copy in copies:
        copy.start()
    for copy in copies:
        copy.wait()


def solution(mesh):
    nc = mesh.shape["ctx"] // 2
    nx = mesh.shape["head"]
    part = 512 // nc

    def body(query_rows, key_rows, value_rows, log_decay, step_size, band_mask, cotangent):
        tok, width = query_rows.shape
        out = jax.ShapeDtypeStruct((tok, width), BF16)
        hbm = pl.BlockSpec(memory_space=pltpu.HBM)
        band = pltpu.VMEM((3, 2, D, HW), BF16)
        tile2 = pltpu.VMEM((2, 8, D), F32)
        share = pltpu.VMEM((nc, part, D), BF16)
        whole = pltpu.VMEM((HW, D), BF16)
        per_head = pltpu.VMEM((HH, T2, D), F32)
        square = pltpu.VMEM((HH, T2, T2), F32)
        results = pl.pallas_call(
            functools.partial(kernel, nc, nx),
            name="mixer",
            out_shape=(pltpu.VMEM((tok, width), BF16),) * 4,
            in_specs=[hbm] * 7,
            out_specs=(pl.BlockSpec(memory_space=pltpu.VMEM),) * 4,
            scratch_shapes=[
                band, band, band, band, pltpu.VMEM((D, HW), BF16), pltpu.VMEM((D, HW), BF16),
                tile2, tile2, tile2, pltpu.VMEM((1, 5), jnp.int32),
                whole, whole, pltpu.VMEM((HW, D), F32), pltpu.VMEM((2, nc, 8, D), F32),
                whole, share, share, whole,
                share, whole, share, whole,
                pltpu.VMEM((2 * nx, 8, T2), F32), pltpu.VMEM((3, 24, T2), F32),
                pltpu.VMEM((16, T2), F32), pltpu.VMEM((T2, 16), F32),
                pltpu.VMEM((8, W3), F32), pltpu.VMEM((8, W3), F32),
                square, square, pltpu.VMEM((HH, T2, T2), BF16), pltpu.VMEM((HH, D, T2), BF16),
                per_head, pltpu.VMEM((HH, T2, D), BF16),
                pltpu.VMEM((HH, T2, W3), F32), pltpu.VMEM((HH, T2, W3), F32),
                per_head, per_head, per_head,
                pltpu.VMEM((4, 2, D, HW), BF16),
                pltpu.SemaphoreType.DMA((80,)), pltpu.SemaphoreType.DMA((80,)),
                pltpu.SemaphoreType.DMA((16,)),
            ],
            compiler_params=pltpu.CompilerParams(
                collective_id=0, has_side_effects=True, vmem_limit_bytes=56 << 20
            ),
        )(
            *[
                pltpu.with_memory_space_constraint(a, pltpu.HBM)
                for a in (
                    query_rows, key_rows, value_rows, cotangent, log_decay, step_size, band_mask
                )
            ]
        )
        return pl.pallas_call(
            store,
            name="store",
            out_shape=(out,) * 4,
            in_specs=[pl.BlockSpec(memory_space=pltpu.VMEM)] * 4,
            out_specs=(hbm,) * 4,
            scratch_shapes=[pltpu.SemaphoreType.DMA((4,))],
        )(*[pltpu.with_memory_space_constraint(a, pltpu.VMEM) for a in results])

    return jax.shard_map(
        body,
        mesh=mesh,
        in_specs=(
            P("ctx", "head"),
            P("ctx", "head"),
            P("ctx", "head"),
            P("head", "ctx"),
            P("head", "ctx"),
            P("ctx", None),
            P("ctx", "head"),
        ),
        out_specs=(P("ctx", "head"), P("ctx", "head"), P("ctx", "head"), P("ctx", "head")),
        check_vma=False,
    )
```
